1024 devices in a mesh: ctx: 16 (over z, core), grp: 64 (over x, y).
Axes of the slice: x: 8, y: 8, z: 8, core: 2. Of those that a mesh axis runs over, the one named last changes fastest.
Arguments:
- latent: bfloat16 [64, 2048, 576], P('grp', 'ctx'), may hold values from -6 to 6
- queries: bfloat16 [64, 64, 73728], P('grp', 'ctx'), may hold values from -4 to 4
- out_grad: bfloat16 [64, 64, 65536], P('grp', 'ctx'), may hold values from -6 to 6
- hidden: bfloat16 [64, 2048, 7168], P('grp', None, 'ctx'), may hold values from -6 to 6
- doc_ids: int32 [64, 2048], P('grp', 'ctx'), may hold values from 0 to 7, never falling along the last dimension, each value on 1 to 1024 neighbouring positions
- clip_limits: float32 [64, 8], P('grp'), may hold values from 0.05 to 20
Outputs:
- grad_keys: bfloat16 [64, 2048, 576], P('grp', 'ctx')
- weight_grad: float32 [576, 7168], P('grp', 'ctx')
The draws below stay inside these ranges and needn't reach their ends.
Inputs may be any that keep to these rules, and one draw needn't show every extreme that they name: `doc_ids`: within each group the ids never fall; each document has 1 to 1024 tokens and one has exactly 1024.
All inputs are finite; a program needn't handle non-finite values.
Results may differ from the reference program's by a relative error of at most 0.0095.
Values may be sent and summed in bfloat16 or wider, within the bound.
No kernel may reach another device: no remote copies, remote signals or barrier semaphores. Data moves between devices by JAX's collectives and lax.ppermute only.
A program may use at most 64 MiB of HBM per device.

```python
import math
import jax
import jax.numpy as jnp
import numpy as np
from jax import lax

D = 7168
LATENT = 512
HEADS = 128
KW = 576
TOK_DEV = 128
Q_DEV = 4
NDOC = 8
SEQ = 2048
MOST = 1024
WIN = 1028
QROWS = 64
GROUPS = 64
N_CTX = 16


def plant_plan(key):
    shards = SEQ // TOK_DEV
    half = KW // 2
    group_keys = jax.random.split(jax.random.fold_in(key, 101), GROUPS)
    orders = jax.vmap(lambda one: jax.random.permutation(one, KW))(group_keys)
    ranks = jnp.argsort(orders, axis=1)
    chosen = ranks < half
    flips = jax.random.bernoulli(jax.random.fold_in(key, 102), 0.5, (GROUPS, shards, KW))
    signs = jnp.where(flips, 1.0, -1.0).astype(jnp.float32)
    strength = 2.5 + 0.5 * jax.random.randint(jax.random.fold_in(key, 103), (GROUPS, shards), 0, 4).astype(jnp.float32)
    head_pick = jax.random.randint(jax.random.fold_in(key, 104), (GROUPS, shards), 0, HEADS)
    return (chosen, signs, strength, head_pick)


def draw_latent(key, part):
    chosen, signs, strength, head_pick = plant_plan(key)
    shards = SEQ // TOK_DEV
    base_key = jax.random.fold_in(key, 201)
    base = jnp.clip(jax.random.normal(base_key, (GROUPS, SEQ, KW), jnp.float32), -6.0, 6.0)
    base = base.reshape(GROUPS, shards, TOK_DEV, KW)
    slot = jnp.arange(TOK_DEV)[None, None, :, None]
    magnitude = jnp.where(slot == TOK_DEV - 1, 5.0, 4.96875).astype(jnp.float32)
    planted = magnitude * signs[:, :, None, :]
    placed = (slot >= TOK_DEV - 2) & chosen[:, None, None, :]
    result = jnp.where(placed, planted, base)
    return result.reshape(GROUPS, SEQ, KW).astype(jnp.bfloat16)


def draw_queries(key, part):
    chosen, signs, strength, head_pick = plant_plan(key)
    shards = SEQ // TOK_DEV
    rows_dev = QROWS // shards
    base_key = jax.random.fold_in(key, 301)
    base = jnp.clip(0.5 * jax.random.normal(base_key, (GROUPS, QROWS, HEADS * KW), jnp.float32), -4.0, 4.0)
    base = base.reshape(GROUPS, shards, rows_dev, HEADS, KW)
    target = strength[:, :, None] * signs * chosen[:, None, :].astype(jnp.float32)
    last_row = (jnp.arange(rows_dev) == rows_dev - 1)[None, None, :, None, None]
    head_hit = (jnp.arange(HEADS)[None, None, :] == head_pick[:, :, None])[:, :, None, :, None]
    result = jnp.where(last_row & head_hit, target[:, :, None, None, :], base)
    return result.reshape(GROUPS, QROWS, HEADS * KW).astype(jnp.bfloat16)


def block_levels(stream_key, extent, cuts, smallest, high):
    def one(dim, blocks):
        steps = jax.random.uniform(jax.random.fold_in(jax.random.fold_in(stream_key, 6), dim), (blocks,), jnp.float32, smallest / len(cuts), high / len(cuts))
        return jnp.repeat(jnp.exp(steps), extent[dim] // blocks).reshape((-1,) + (1,) * (len(extent) - dim - 1))

    gain = one(*cuts[0])
    for cut in cuts[1:]:
        gain = gain * one(*cut)
    return gain


def length_profile(count, total, bound, skew):
    portions = [(1 << 20) // math.isqrt(standing ** skew) + 1 for standing in range(2, count + 1)]
    spare, counts = total - bound - (count - 1), [1] * (count - 1)
    while spare > 0:
        movable = [i for i in range(count - 1) if counts[i] < bound]
        whole, remaining = sum([portions[i] for i in movable]), spare
        for i in movable:
            addition = min(bound - counts[i], max(1, remaining * portions[i] // whole), spare)
            counts[i] = counts[i] + addition
            spare = spare - addition
    return np.array([bound] + counts)


def uneven_parts(own_key, number_of, total, limit, slope):
    if number_of == 2:
        one = jax.random.randint(own_key, (), max(1, total - limit), min(limit, total - 1) + 1)
        return jnp.stack([one, total - one])
    sizes = jnp.asarray(length_profile(number_of, total, limit, slope), jnp.int32)
    pairs = (number_of - 1) // 2
    donor, sink = sizes[1:1 + 2 * pairs:2], sizes[2:2 + 2 * pairs:2]
    slack = jnp.minimum(donor - 1, limit - sink)
    passed = jax.random.randint(jax.random.fold_in(own_key, 1), (pairs,), 0, 1 << 20) % (slack + 1)
    sizes = sizes.at[1:1 + 2 * pairs:2].set(donor - passed).at[2:2 + 2 * pairs:2].set(sink + passed)
    return sizes[jax.random.permutation(jax.random.fold_in(own_key, 2), number_of)]


def normal_values(key, extent, width, most, cuts=(), kind=jnp.bfloat16):
    values = jax.random.normal(key, extent, jnp.float32) * width
    if len(cuts) > 0:
        values = block_levels(key, extent, cuts, -0.22, 0.18) * values
    return jnp.clip(values, min=-most, max=most).astype(kind)


def setup_inputs(seed: int = 0) -> dict:
    streams_of = jax.random.split(jax.random.key(seed), 7)
    return {
        "latent": draw_latent(jax.random.fold_in(streams_of[6], 71), 0),
        "queries": draw_queries(jax.random.fold_in(streams_of[6], 71), 0),
        "out_grad": normal_values(streams_of[2], (GROUPS, QROWS, HEADS * LATENT), 1.0, 6.0, ((0, 64), (1, 16))),
        "hidden": normal_values(streams_of[3], (GROUPS, SEQ, D), 1.0, 6.0, ((0, 64), (2, 16))),
        "doc_ids": jax.vmap(lambda own: jnp.searchsorted(jnp.cumsum(uneven_parts(own, NDOC, SEQ, MOST, 2)), jnp.arange(SEQ), side="right"))(jax.random.split(streams_of[4], GROUPS)).reshape((GROUPS, SEQ)).astype(jnp.int32),
        "clip_limits": jnp.clip(jnp.exp(math.log(20.0) - 5.9914645 * jax.random.uniform(streams_of[5], (GROUPS, NDOC), jnp.float32) ** block_levels(streams_of[5], (GROUPS, NDOC), ((0, 64),), -0.2, 0.2)), 0.05, 20.0),
    }


score_scale = 192.0 ** (-0.5)
norm_eps = 1e-06

def device_part(latent_g, queries_g, grads_g, ids_g, index):
    first_query = (index * TOK_DEV + TOK_DEV - Q_DEV).astype(jnp.int32)
    start = jnp.clip(first_query + Q_DEV - WIN, 0, SEQ - WIN).astype(jnp.int32)
    query_block = lax.dynamic_slice_in_dim(queries_g, (index * Q_DEV).astype(jnp.int32), Q_DEV, 0)
    query_block = query_block.reshape(Q_DEV, HEADS, KW).astype(jnp.float32)
    grad_block = lax.dynamic_slice_in_dim(grads_g, (index * Q_DEV).astype(jnp.int32), Q_DEV, 0)
    grad_block = grad_block.reshape(Q_DEV, HEADS, LATENT).astype(jnp.float32)
    window_keys = lax.dynamic_slice_in_dim(latent_g, start, WIN, 0).astype(jnp.float32)
    window_ids = lax.dynamic_slice_in_dim(ids_g, start, WIN, 0)
    key_pos = start + jnp.arange(WIN, dtype=jnp.int32)
    query_pos = first_query + jnp.arange(Q_DEV, dtype=jnp.int32)
    query_ids = lax.dynamic_slice_in_dim(ids_g, first_query, Q_DEV, 0)
    allowed = (window_ids[None, :] == query_ids[:, None]) & (key_pos[None, :] <= query_pos[:, None])
    scores = jnp.einsum('qhc,kc->qhk', query_block, window_keys) * score_scale
    scores = jnp.where(allowed[:, None, :], scores, -1e+30)
    top_score = lax.optimization_barrier(jnp.max(scores, axis=-1, keepdims=True))
    weights = jnp.exp(scores - top_score)
    weights = weights / lax.optimization_barrier(jnp.sum(weights, axis=-1, keepdims=True))
    prob_grad = jnp.einsum('qhc,kc->qhk', grad_block, window_keys[:, :LATENT])
    row_dots = lax.optimization_barrier(jnp.sum(weights * prob_grad, axis=-1, keepdims=True))
    score_grad = (weights * (prob_grad - row_dots) * score_scale).astype(jnp.bfloat16).astype(jnp.float32)
    weights_low = weights.astype(jnp.bfloat16).astype(jnp.float32)
    key_grad = jnp.einsum('qhk,qhc->kc', score_grad, query_block)
    value_grad = jnp.einsum('qhk,qhc->kc', weights_low, grad_block)
    key_grad = key_grad.at[:, :LATENT].add(value_grad)
    full = lax.dynamic_update_slice(jnp.zeros((SEQ, KW), jnp.float32), key_grad, (start, jnp.int32(0)))
    return full.astype(jnp.bfloat16)

def reference(latent, queries, out_grad, hidden, doc_ids, clip_limits):

    def per_group(total, group):
        latent_g, queries_g, grads_g, hidden_g, ids_g, limits_g = group
        parts = lax.map(lambda index: device_part(latent_g, queries_g, grads_g, ids_g, index), jnp.arange(N_CTX, dtype=jnp.int32))
        grad_keys = lax.optimization_barrier(jnp.sum(parts.astype(jnp.float32), axis=0)).astype(jnp.bfloat16)
        values = grad_keys.astype(jnp.float32)
        member = (ids_g[:, None] == jnp.arange(NDOC, dtype=jnp.int32)[None, :]).astype(jnp.float32)
        norms = lax.optimization_barrier(jnp.sum(member * lax.optimization_barrier(jnp.sum(values * values, axis=1))[:, None], axis=0))
        factor = jnp.minimum(1.0, limits_g / jnp.sqrt(norms + norm_eps))
        scaled = (values * lax.optimization_barrier(jnp.sum(member * factor[None, :], axis=1))[:, None]).astype(jnp.bfloat16)
        term = jnp.dot(scaled.T, hidden_g, preferred_element_type=jnp.float32)
        return (total + term, grad_keys)
    weight_grad, grad_keys = lax.scan(per_group, jnp.zeros((KW, D), jnp.float32), (latent, queries, out_grad, hidden, doc_ids, clip_limits))
    return (grad_keys, weight_grad)
```

```python
import functools

import jax
import jax.numpy as jnp
from jax import lax
from jax.experimental import pallas as pl
from jax.experimental.pallas import tpu as pltpu
from jax.sharding import PartitionSpec as P

LATENT = 512
KW = 576
HEADS = 128
TOK = 128
Q_DEV = 4
NDOC = 8
CHIPS = 8
BACK = 5
ROWS = 592
PAIR = 2 * TOK
QH = Q_DEV * HEADS
SLOT = 512
GRP_ROWS = 9
TAIL = 56

score_scale = 192.0 ** (-0.5)
norm_eps = 1e-06
VMEM_BYTES = 56 * 1024 * 1024


def chip_shift(value, by0, by1):
    pairs = []
    for chip in range(CHIPS):
        for core, by in ((0, by0), (1, by1)):
            if by is not None:
                pairs.append((2 * chip + core, 2 * ((chip + by) % CHIPS) + core))
    return lax.ppermute(value, "ctx", pairs)


def core_swap(value):
    return lax.ppermute(value, "ctx", [(i, i ^ 1) for i in range(2 * CHIPS)])


def attention_kernel(
    info, o0, o1, o2, o3, o4, p0, p1, p2, p3, p4, rows_ref, cols_ref,
    keep_ref, send_ref, mid_ref, keys, score, dprob, mixed,
):
    chip, core = info[0], info[1]
    own, par = (o0, o1, o2, o3, o4), (p0, p1, p2, p3, p4)

    @pl.when(core == 0)
    def _():
        for k in range(BACK):
            keys[k, :, :TOK] = own[k][...]
            keys[k, :, TOK:] = par[k][...]

    @pl.when(core != 0)
    def _():
        for k in range(BACK):
            keys[k, :, :TOK] = par[k][...]
            keys[k, :, TOK:] = own[k][...]

    own_ids = o0[KW:ROWS, :].astype(jnp.float32)[0:1]
    lane = lax.broadcasted_iota(jnp.int32, (1, TOK), 1)
    query_ids = [
        jnp.sum(jnp.where(lane == TOK - Q_DEV + i, own_ids, 0.0), axis=1, keepdims=True)
        for i in range(Q_DEV)
    ]
    pair_lane = lax.broadcasted_iota(jnp.int32, (1, PAIR), 1)
    tops = [None] * Q_DEV
    for k in range(BACK):
        both = jnp.dot(rows_ref[...], keys[k, :KW, :], preferred_element_type=jnp.float32)
        ids = keys[k, KW:ROWS, :].astype(jnp.float32)[0:1]
        place = pair_lane - k * PAIR
        there = chip - k >= 0
        for i in range(Q_DEV):
            at = core * TOK + TOK - Q_DEV + i
            allowed = (ids == query_ids[i]) & (place <= at) & there
            part = slice(i * HEADS, (i + 1) * HEADS)
            s = jnp.where(allowed, both[part] * score_scale, -1e30)
            score[k, part, :] = s
            tops[i] = s if k == 0 else jnp.maximum(tops[i], s)
        dprob[k] = both[QH:]
    for i in range(Q_DEV):
        part = slice(i * HEADS, (i + 1) * HEADS)
        top = jnp.max(tops[i], axis=1, keepdims=True)
        total = dots = None
        for k in range(BACK):
            e = jnp.exp(score[k, part, :] - top)
            score[k, part, :] = e
            w = e * dprob[k, part, :]
            total = e if k == 0 else total + e
            dots = w if k == 0 else dots + w
        inv = 1.0 / jnp.sum(total, axis=1, keepdims=True)
        row_dot = jnp.sum(dots, axis=1, keepdims=True) * inv
        for k in range(BACK):
            prob = score[k, part, :] * inv
            grad = prob * (dprob[k, part, :] - row_dot) * score_scale
            mixed[k, part, :] = grad.astype(jnp.bfloat16)
            mixed[k, QH + i * HEADS : QH + (i + 1) * HEADS, :] = prob.astype(jnp.bfloat16)

    blank = jnp.zeros((ROWS - KW, PAIR), jnp.bfloat16)
    for slot in range(2):
        keep_ref[slot, KW:, :] = blank
        send_ref[slot, KW:, :] = blank
    mid_ref[KW:, :] = (keys[2, KW:ROWS, :].astype(jnp.float32) * 0.5).astype(jnp.bfloat16)
    for k in range(BACK):
        g = jnp.dot(cols_ref[...], mixed[k], preferred_element_type=jnp.float32)
        g = g.astype(jnp.bfloat16)
        if k == 2:
            mid_ref[:KW, :] = g
            continue
        slot, keeper = (k, 0) if k < 2 else (4 - k, 1)

        @pl.when(core == keeper)
        def _():
            keep_ref[slot, :KW, :] = g

        @pl.when(core != keeper)
        def _():
            send_ref[slot, :KW, :] = g


def vmem():
    return pl.BlockSpec(memory_space=pltpu.VMEM)


def smem():
    return pl.BlockSpec(memory_space=pltpu.SMEM)


def attention(info, own, par, rows, cols):
    block = jax.ShapeDtypeStruct((2, ROWS, PAIR), jnp.bfloat16)
    return pl.pallas_call(
        attention_kernel,
        out_shape=(block, block, jax.ShapeDtypeStruct((ROWS, PAIR), jnp.bfloat16)),
        in_specs=[smem()] + [vmem()] * 12,
        out_specs=(vmem(), vmem(), vmem()),
        scratch_shapes=[
            pltpu.VMEM((BACK, ROWS, PAIR), jnp.bfloat16),
            pltpu.VMEM((BACK, QH, PAIR), jnp.float32),
            pltpu.VMEM((BACK, QH, PAIR), jnp.float32),
            pltpu.VMEM((BACK, 2 * QH, PAIR), jnp.bfloat16),
        ],
        compiler_params=pltpu.CompilerParams(vmem_limit_bytes=VMEM_BYTES),
        name="attention_grads",
    )(info, *own, *par, rows, cols)


def down_kernel(
    info, limits, g0, r1, r2, r3, s1, s2, s3, r4, s4, hidden,
    out_ref, own_ref, last, scaled, weight,
):
    chip, core = info[0], info[1]

    @pl.when(core == 0)
    def _():
        last[:, :TOK] = r4[...]
        last[:, TOK:] = s4[...]
        own_ref[...] = s2[:KW, :TOK]

    @pl.when(core != 0)
    def _():
        last[:, :TOK] = s4[...]
        last[:, TOK:] = r4[...]
        own_ref[...] = r2[:KW, TOK:]

    away = jnp.where(core == 0, -1, 1)
    blocks = [(g0, 0)]
    blocks += [(r, away * (j + 1)) for j, r in enumerate((r1, r2, r3))]
    blocks += [(s, -away * (j + 1)) for j, s in enumerate((s1, s2, s3))]
    blocks += [(last, 4)]
    doc = lax.broadcasted_iota(jnp.int32, (NDOC, PAIR), 0).astype(jnp.float32)
    squares = jnp.zeros((NDOC, PAIR), jnp.float32)
    members = []
    for ref, _ in blocks:
        x = ref[:KW, :].astype(jnp.float32)
        ids = ref[KW:ROWS, :].astype(jnp.float32)[0:1]
        member = doc == ids
        members.append(member)
        squares = squares + jnp.where(member, jnp.sum(x * x, axis=0, keepdims=True), 0.0)
    norms = jnp.sum(squares, axis=1, keepdims=True)
    factor = jnp.minimum(1.0, limits[:, 0:1] / jnp.sqrt(norms + norm_eps))
    for (ref, by), member in zip(blocks, members, strict=True):
        gain = jnp.sum(jnp.where(member, factor, 0.0), axis=0, keepdims=True)
        shard = lax.rem(chip + by + 2 * CHIPS - 2, CHIPS)
        x = ref[:KW, :].astype(jnp.float32) * gain
        scaled[:, pl.ds(pl.multiple_of(shard * PAIR, PAIR), PAIR)] = x.astype(jnp.bfloat16)
    product = lax.dot_general(
        scaled[...], hidden[...], (((1,), (1,)), ((), ())), preferred_element_type=jnp.float32
    )
    width = product.shape[1]
    weight[...] = jnp.zeros_like(weight)
    weight[:, :width] = product.astype(jnp.bfloat16)
    whole = weight[...]
    row = lax.broadcasted_iota(jnp.int32, (SLOT, KW), 0)
    col = lax.broadcasted_iota(jnp.int32, (SLOT, KW), 1)
    pick = (col == row + lax.shift_right_logical(row, 3)).astype(jnp.bfloat16)
    first = jnp.dot(pick, whole, preferred_element_type=jnp.float32)
    row = lax.broadcasted_iota(jnp.int32, (SLOT // 8, KW), 0)
    col = lax.broadcasted_iota(jnp.int32, (SLOT // 8, KW), 1)
    pick = (col == row * GRP_ROWS + 8).astype(jnp.bfloat16)
    ninth = jnp.dot(pick, whole, preferred_element_type=jnp.float32).astype(jnp.bfloat16)
    row = lax.broadcasted_iota(jnp.int32, (SLOT, 128), 0)
    col = lax.broadcasted_iota(jnp.int32, (SLOT, 128), 1)
    pieces = []
    for s in range(8):
        pick = ((row == col - 64 + s * TAIL) & (col >= 64) & (col < 64 + TAIL)).astype(jnp.bfloat16)
        pieces.append(
            jnp.dot(ninth, pick, preferred_element_type=jnp.float32).astype(jnp.bfloat16)
        )
    pieces = jnp.concatenate(pieces, axis=0)
    row = lax.broadcasted_iota(jnp.int32, (SLOT, SLOT), 0)
    col = lax.broadcasted_iota(jnp.int32, (SLOT, SLOT), 1)
    pick = (col == (row & 7) * 64 + lax.shift_right_logical(row, 3)).astype(jnp.bfloat16)
    tail = jnp.dot(pick, pieces, preferred_element_type=jnp.float32)
    out_ref[:, :384] = first[:, :384].astype(jnp.bfloat16)
    out_ref[:, 384:] = (first[:, 384:] + tail).astype(jnp.bfloat16)


def down_grad(info, limits, blocks, hidden):
    return pl.pallas_call(
        down_kernel,
        out_shape=(
            jax.ShapeDtypeStruct((SLOT, SLOT), jnp.bfloat16),
            jax.ShapeDtypeStruct((KW, TOK), jnp.bfloat16),
        ),
        in_specs=[smem()] + [vmem()] * 11,
        out_specs=(vmem(), vmem()),
        scratch_shapes=[
            pltpu.VMEM((ROWS, PAIR), jnp.bfloat16),
            pltpu.VMEM((KW, CHIPS * PAIR), jnp.bfloat16),
            pltpu.VMEM((KW, SLOT), jnp.bfloat16),
        ],
        compiler_params=pltpu.CompilerParams(vmem_limit_bytes=VMEM_BYTES),
        name="down_grad",
    )(info, limits, *blocks, hidden)


def added(*terms):
    total = terms[0].astype(jnp.float32)
    for term in terms[1:]:
        total = total + term.astype(jnp.float32)
    return total.astype(jnp.bfloat16)


def group_part(latent, queries, out_grad, hidden, doc_ids, clip_limits):
    position = lax.axis_index("ctx")
    core = position % 2
    info = jnp.stack([position // 2, core]).astype(jnp.int32)
    ids = jnp.pad(doc_ids.astype(jnp.bfloat16), ((0, ROWS - KW - 1), (0, 0)))
    keys = jnp.concatenate([latent[0].T, ids], axis=0)
    own = [keys, chip_shift(keys, 1, 1), chip_shift(keys, 2, 2), chip_shift(keys, 3, 3)]
    own.append(chip_shift(chip_shift(keys, -2, -2), -2, -2))
    par = [core_swap(value) for value in own]
    query_rows = queries[0].reshape(QH, KW)
    grad_rows = out_grad[0].reshape(QH, LATENT)
    rows = jnp.concatenate([query_rows, jnp.pad(grad_rows, ((0, 0), (0, KW - LATENT)))], axis=0)
    keep, send, mid = attention(info, own, par, rows, rows.T)

    arrived = core_swap(send)
    moved = chip_shift(added(keep[0], arrived[0]), 1, -1)
    moved = chip_shift(added(keep[1], arrived[1], moved), 1, -1)
    mine = added(mid, moved)
    total = added(mine, core_swap(mine))

    ring = [total]
    for _ in range(3):
        ring.append(chip_shift(ring[-1], 1, -1))
    half = jnp.where(core == 0, ring[3][:, :TOK], ring[3][:, TOK:])
    ring.append(chip_shift(half, 1, -1))
    swapped = [core_swap(value) for value in ring[1:]]
    limits = jnp.broadcast_to(clip_limits[0][:, None], (NDOC, 128))
    blocks = ring[:4] + swapped[:3] + [ring[4], swapped[3]]
    chunks, own_grad = down_grad(info, limits, blocks, hidden[0].T)
    return own_grad, chunks


def on_device(latent, queries, out_grad, hidden, doc_ids, clip_limits):
    own_grad, chunks = group_part(latent, queries, out_grad, hidden, doc_ids, clip_limits)
    groups = lax.axis_size("grp")
    chunks = chunks.reshape(groups, SLOT // groups, SLOT)
    chunks = lax.all_to_all(chunks, "grp", 0, 0, tiled=True)
    mine = jnp.sum(chunks.astype(jnp.float32), axis=0)
    width = hidden.shape[2]
    ninth = mine[:, width : width + TAIL].reshape(1, width)
    weight_grad = jnp.concatenate([mine[:, :width], ninth], axis=0)
    return own_grad.T[None], weight_grad


def solution(mesh):
    return jax.shard_map(
        on_device,
        mesh=mesh,
        in_specs=(
            P("grp", "ctx", None),
            P("grp", "ctx", None),
            P("grp", "ctx", None),
            P("grp", None, "ctx"),
            P("grp", "ctx"),
            P("grp", None),
        ),
        out_specs=(P("grp", "ctx", None), P("grp", "ctx")),
        check_vma=False,
    )
```

```python
import functools

import jax
import jax.numpy as jnp
from jax import lax
from jax.experimental import pallas as pl
from jax.experimental.pallas import tpu as pltpu
from jax.sharding import PartitionSpec as P

LATENT = 512
KW = 576
HEADS = 128
TOK = 128
Q_DEV = 4
NDOC = 8
CHIPS = 8
BACK = 5
ROWS = 592
PAIR = 2 * TOK
QH = Q_DEV * HEADS
SLOT = 512
GRP_ROWS = 9
TAIL = 56

score_scale = 192.0 ** (-0.5)
norm_eps = 1e-06
VMEM_BYTES = 56 * 1024 * 1024


def chip_shift(value, by0, by1):
    pairs = []
    for chip in range(CHIPS):
        for core, by in ((0, by0), (1, by1)):
            if by is not None:
                pairs.append((2 * chip + core, 2 * ((chip + by) % CHIPS) + core))
    return lax.ppermute(value, "ctx", pairs)


def core_swap(value):
    return lax.ppermute(value, "ctx", [(i, i ^ 1) for i in range(2 * CHIPS)])


def attention_kernel(
    info, own, par, rows_ref, cols_ref,
    keep_ref, send_ref, mid_ref, keys, score, dprob, mixed,
):
    chip, core = info[0], info[1]

    mine = pl.ds(pl.multiple_of(core * TOK, TOK), TOK)
    other = pl.ds(pl.multiple_of((1 - core) * TOK, TOK), TOK)
    for k in range(BACK):
        keys[k, :, mine] = own[k]
        keys[k, :, other] = par[k]

    own_ids = own[0, KW:ROWS, :].astype(jnp.float32)[0:1]
    lane = lax.broadcasted_iota(jnp.int32, (1, TOK), 1)
    query_ids = [
        jnp.sum(jnp.where(lane == TOK - Q_DEV + i, own_ids, 0.0), axis=1, keepdims=True)
        for i in range(Q_DEV)
    ]
    pair_lane = lax.broadcasted_iota(jnp.int32, (1, PAIR), 1)
    tops = [None] * Q_DEV
    for k in range(BACK):
        both = jnp.dot(rows_ref[...], keys[k, :KW, :], preferred_element_type=jnp.float32)
        ids = keys[k, KW:ROWS, :].astype(jnp.float32)[0:1]
        place = pair_lane - k * PAIR
        there = chip - k >= 0
        for i in range(Q_DEV):
            at = core * TOK + TOK - Q_DEV + i
            allowed = (ids == query_ids[i]) & (place <= at) & there
            part = slice(i * HEADS, (i + 1) * HEADS)
            s = jnp.where(allowed, both[part] * score_scale, -1e30)
            score[k, part, :] = s
            tops[i] = s if k == 0 else jnp.maximum(tops[i], s)
        dprob[k] = both[QH:]
    for i in range(Q_DEV):
        part = slice(i * HEADS, (i + 1) * HEADS)
        top = jnp.max(tops[i], axis=1, keepdims=True)
        total = dots = None
        for k in range(BACK):
            e = jnp.exp(score[k, part, :] - top)
            score[k, part, :] = e
            w = e * dprob[k, part, :]
            total = e if k == 0 else total + e
            dots = w if k == 0 else dots + w
        inv = 1.0 / jnp.sum(total, axis=1, keepdims=True)
        row_dot = jnp.sum(dots, axis=1, keepdims=True) * inv
        for k in range(BACK):
            prob = score[k, part, :] * inv
            grad = prob * (dprob[k, part, :] - row_dot) * score_scale
            mixed[k, part, :] = grad.astype(jnp.bfloat16)
            mixed[k, QH + i * HEADS : QH + (i + 1) * HEADS, :] = prob.astype(jnp.bfloat16)

    blank = jnp.zeros((ROWS - KW, PAIR), jnp.bfloat16)
    for slot in range(2):
        keep_ref[slot, KW:, :] = blank
        send_ref[slot, KW:, :] = blank
    mid_ref[KW:, :] = (keys[2, KW:ROWS, :].astype(jnp.float32) * 0.5).astype(jnp.bfloat16)

    def grads(k):
        g = jnp.dot(cols_ref[...], mixed[k], preferred_element_type=jnp.float32)
        return g.astype(jnp.bfloat16)

    for slot in range(2):
        send_ref[slot, :KW, :] = grads(jnp.where(core == 0, 4 - slot, slot))
    for slot in range(2):
        keep_ref[slot, :KW, :] = grads(jnp.where(core == 0, slot, 4 - slot))
    mid_ref[:KW, :] = grads(2)


def vmem():
    return pl.BlockSpec(memory_space=pltpu.VMEM)


def smem():
    return pl.BlockSpec(memory_space=pltpu.SMEM)


def attention(info, own, par, rows, cols):
    block = jax.ShapeDtypeStruct((2, ROWS, PAIR), jnp.bfloat16)
    return pl.pallas_call(
        attention_kernel,
        out_shape=(block, block, jax.ShapeDtypeStruct((ROWS, PAIR), jnp.bfloat16)),
        in_specs=[smem()] + [vmem()] * 4,
        out_specs=(vmem(), vmem(), vmem()),
        scratch_shapes=[
            pltpu.VMEM((BACK, ROWS, PAIR), jnp.bfloat16),
            pltpu.VMEM((BACK, QH, PAIR), jnp.float32),
            pltpu.VMEM((BACK, QH, PAIR), jnp.float32),
            pltpu.VMEM((BACK, 2 * QH, PAIR), jnp.bfloat16),
        ],
        compiler_params=pltpu.CompilerParams(vmem_limit_bytes=VMEM_BYTES),
        name="attention_grads",
    )(info, own, par, rows, cols)


def down_kernel(
    info, limits, g0, r12, r34, s12, s34, hidden, out_ref, own_ref, last, scaled, weight,
):
    chip, core = info[0], info[1]
    mine = pl.ds(pl.multiple_of(core * TOK, TOK), TOK)
    other = pl.ds(pl.multiple_of((1 - core) * TOK, TOK), TOK)
    last[:, mine] = r34[:, PAIR:]
    last[:, other] = s34[:, PAIR:]

    @pl.when(core == 0)
    def _():
        own_ref[...] = s12[1, :KW, :TOK]

    @pl.when(core != 0)
    def _():
        own_ref[...] = r12[1, :KW, TOK:]

    away = jnp.where(core == 0, -1, 1)
    blocks = [(g0, 0), (r12.at[0], away), (r12.at[1], 2 * away), (r34.at[:, :PAIR], 3 * away)]
    blocks += [(s12.at[0], -away), (s12.at[1], -2 * away), (s34.at[:, :PAIR], -3 * away)]
    blocks += [(last, 4)]
    doc = lax.broadcasted_iota(jnp.int32, (NDOC, PAIR), 0).astype(jnp.float32)
    squares = jnp.zeros((NDOC, PAIR), jnp.float32)
    members = []
    for ref, _ in blocks:
        x = ref[:KW, :].astype(jnp.float32)
        ids = ref[KW:ROWS, :].astype(jnp.float32)[0:1]
        member = doc == ids
        members.append(member)
        squares = squares + jnp.where(member, jnp.sum(x * x, axis=0, keepdims=True), 0.0)
    norms = jnp.sum(squares, axis=1, keepdims=True)
    factor = jnp.minimum(1.0, limits[:, 0:1] / jnp.sqrt(norms + norm_eps))
    for (ref, by), member in zip(blocks, members, strict=True):
        gain = jnp.sum(jnp.where(member, factor, 0.0), axis=0, keepdims=True)
        shard = lax.rem(chip + by + 2 * CHIPS - 2, CHIPS)
        x = ref[:KW, :].astype(jnp.float32) * gain
        scaled[:, pl.ds(pl.multiple_of(shard * PAIR, PAIR), PAIR)] = x.astype(jnp.bfloat16)
    product = lax.dot_general(
        scaled[...], hidden[...], (((1,), (1,)), ((), ())), preferred_element_type=jnp.float32
    )
    width = product.shape[1]
    weight[...] = jnp.zeros_like(weight)
    weight[:, :width] = product.astype(jnp.bfloat16)
    whole = weight[...]
    row = lax.broadcasted_iota(jnp.int32, (SLOT, KW), 0)
    col = lax.broadcasted_iota(jnp.int32, (SLOT, KW), 1)
    pick = (col == row + lax.shift_right_logical(row, 3)).astype(jnp.bfloat16)
    first = jnp.dot(pick, whole, preferred_element_type=jnp.float32)
    row = lax.broadcasted_iota(jnp.int32, (SLOT // 8, KW), 0)
    col = lax.broadcasted_iota(jnp.int32, (SLOT // 8, KW), 1)
    pick = (col == row * GRP_ROWS + 8).astype(jnp.bfloat16)
    ninth = jnp.dot(pick, whole, preferred_element_type=jnp.float32).astype(jnp.bfloat16)
    row = lax.broadcasted_iota(jnp.int32, (SLOT, 128), 0)
    col = lax.broadcasted_iota(jnp.int32, (SLOT, 128), 1)
    pieces = []
    for s in range(8):
        pick = ((row == col - 64 + s * TAIL) & (col >= 64) & (col < 64 + TAIL)).astype(jnp.bfloat16)
        pieces.append(
            jnp.dot(ninth, pick, preferred_element_type=jnp.float32).astype(jnp.bfloat16)
        )
    pieces = jnp.concatenate(pieces, axis=0)
    row = lax.broadcasted_iota(jnp.int32, (SLOT, SLOT), 0)
    col = lax.broadcasted_iota(jnp.int32, (SLOT, SLOT), 1)
    pick = (col == (row & 7) * 64 + lax.shift_right_logical(row, 3)).astype(jnp.bfloat16)
    tail = jnp.dot(pick, pieces, preferred_element_type=jnp.float32)
    out_ref[:, :384] = first[:, :384].astype(jnp.bfloat16)
    out_ref[:, 384:] = (first[:, 384:] + tail).astype(jnp.bfloat16)


def down_grad(info, limits, blocks, hidden):
    return pl.pallas_call(
        down_kernel,
        out_shape=(
            jax.ShapeDtypeStruct((SLOT, SLOT), jnp.bfloat16),
            jax.ShapeDtypeStruct((KW, TOK), jnp.bfloat16),
        ),
        in_specs=[smem()] + [vmem()] * 7,
        out_specs=(vmem(), vmem()),
        scratch_shapes=[
            pltpu.VMEM((ROWS, PAIR), jnp.bfloat16),
            pltpu.VMEM((KW, CHIPS * PAIR), jnp.bfloat16),
            pltpu.VMEM((KW, SLOT), jnp.bfloat16),
        ],
        compiler_params=pltpu.CompilerParams(vmem_limit_bytes=VMEM_BYTES),
        name="down_grad",
    )(info, limits, *blocks, hidden)


def added(*terms):
    total = terms[0].astype(jnp.float32)
    for term in terms[1:]:
        total = total + term.astype(jnp.float32)
    return total.astype(jnp.bfloat16)


def group_part(latent, queries, out_grad, hidden, doc_ids, clip_limits):
    position = lax.axis_index("ctx")
    core = position % 2
    info = jnp.stack([position // 2, core]).astype(jnp.int32)
    ids = jnp.pad(doc_ids.astype(jnp.bfloat16), ((0, ROWS - KW - 1), (0, 0)))
    keys = jnp.concatenate([latent[0].T, ids], axis=0)
    near = chip_shift(keys, 1, 1)
    fourth = chip_shift(keys, 4, 4)
    next_near = chip_shift(keys, 2, 2)
    next_near, query_rows, grad_rows = lax.optimization_barrier((next_near, queries, out_grad))
    query_rows = query_rows[0].reshape(QH, KW)
    grad_rows = grad_rows[0].reshape(QH, LATENT)
    rows = jnp.concatenate([query_rows, jnp.pad(grad_rows, ((0, 0), (0, KW - LATENT)))], axis=0)
    cols = rows.T
    limits = jnp.broadcast_to(clip_limits[0][:, None], (NDOC, 128))
    own = jnp.stack([keys, near, next_near, chip_shift(near, 2, 2), fourth])
    own, rows, cols, info, limits = lax.optimization_barrier((own, rows, cols, info, limits))
    par = core_swap(own)
    keep, send, mid = attention(info, own, par, rows, cols)

    arrived = core_swap(send)
    far = chip_shift(added(keep[0], arrived[0]), 2, -2)
    close = chip_shift(added(keep[1], arrived[1]), 1, -1)
    mine = added(mid, far, close)
    total = added(mine, core_swap(mine))

    one = chip_shift(total, 1, -1)
    two = chip_shift(total, 2, -2)
    three = chip_shift(one, 2, -2)
    half = jnp.where(core == 0, two[:, :TOK], two[:, TOK:])
    four = chip_shift(half, 2, -2)
    one, two, three = lax.optimization_barrier((one, two, three))
    nearer = jnp.stack([one, two])
    nearer_par = core_swap(nearer)
    farther = jnp.concatenate([three, four], axis=1)
    blocks = [total, nearer, farther, nearer_par, core_swap(farther)]
    chunks, own_grad = down_grad(info, limits, blocks, hidden[0].T)
    return own_grad, chunks


def on_device(latent, queries, out_grad, hidden, doc_ids, clip_limits):
    own_grad, chunks = group_part(latent, queries, out_grad, hidden, doc_ids, clip_limits)
    groups = lax.axis_size("grp")
    chunks = chunks.reshape(groups, SLOT // groups, SLOT)
    chunks = lax.all_to_all(chunks, "grp", 0, 0, tiled=True)
    mine = jnp.sum(chunks.astype(jnp.float32), axis=0)
    width = hidden.shape[2]
    ninth = mine[:, width : width + TAIL].reshape(1, width)
    weight_grad = jnp.concatenate([mine[:, :width], ninth], axis=0)
    return own_grad.T[None], weight_grad


def solution(mesh):
    return jax.shard_map(
        on_device,
        mesh=mesh,
        in_specs=(
            P("grp", "ctx", None),
            P("grp", "ctx", None),
            P("grp", "ctx", None),
            P("grp", None, "ctx"),
            P("grp", "ctx"),
            P("grp", None),
        ),
        out_specs=(P("grp", "ctx", None), P("grp", "ctx")),
        check_vma=False,
    )
```

```python
import functools

import jax
import jax.numpy as jnp
from jax import lax
from jax.experimental import pallas as pl
from jax.experimental.pallas import tpu as pltpu
from jax.sharding import PartitionSpec as P

LATENT = 512
KW = 576
HEADS = 128
TOK = 128
Q_DEV = 4
NDOC = 8
CHIPS = 8
BACK = 5
ROWS = 592
PAIR = 2 * TOK
QH = Q_DEV * HEADS
SLOT = 512
GRP_ROWS = 9
TAIL = 56

score_scale = 192.0 ** (-0.5)
norm_eps = 1e-06
MIB = 1024 * 1024


def chip_shift(value, by0, by1):
    pairs = []
    for chip in range(CHIPS):
        for core, by in ((0, by0), (1, by1)):
            if by is not None:
                pairs.append((2 * chip + core, 2 * ((chip + by) % CHIPS) + core))
    return lax.ppermute(value, "ctx", pairs)


def core_swap(value):
    return lax.ppermute(value, "ctx", [(i, i ^ 1) for i in range(2 * CHIPS)])


def attention_kernel(
    info, own, par, rows_ref, cols_ref,
    keep_ref, send_ref, mid_ref, keys, score, dprob, mixed,
):
    chip, core = info[0], info[1]

    mine = pl.ds(pl.multiple_of(core * TOK, TOK), TOK)
    other = pl.ds(pl.multiple_of((1 - core) * TOK, TOK), TOK)
    for k in range(BACK):
        keys[k, :, mine] = own[k]
        keys[k, :, other] = par[k]

    own_ids = own[0, KW:ROWS, :].astype(jnp.float32)[0:1]
    lane = lax.broadcasted_iota(jnp.int32, (1, TOK), 1)
    query_ids = [
        jnp.sum(jnp.where(lane == TOK - Q_DEV + i, own_ids, 0.0), axis=1, keepdims=True)
        for i in range(Q_DEV)
    ]
    pair_lane = lax.broadcasted_iota(jnp.int32, (1, PAIR), 1)
    tops = [None] * Q_DEV
    for k in range(BACK):
        both = jnp.dot(rows_ref[...], keys[k, :KW, :], preferred_element_type=jnp.float32)
        ids = keys[k, KW:ROWS, :].astype(jnp.float32)[0:1]
        place = pair_lane - k * PAIR
        there = chip - k >= 0
        for i in range(Q_DEV):
            at = core * TOK + TOK - Q_DEV + i
            allowed = (ids == query_ids[i]) & (place <= at) & there
            part = slice(i * HEADS, (i + 1) * HEADS)
            s = jnp.where(allowed, both[part] * score_scale, -1e30)
            score[k, part, :] = s
            tops[i] = s if k == 0 else jnp.maximum(tops[i], s)
        dprob[k] = both[QH:]
    for i in range(Q_DEV):
        part = slice(i * HEADS, (i + 1) * HEADS)
        top = jnp.max(tops[i], axis=1, keepdims=True)
        total = dots = None
        for k in range(BACK):
            e = jnp.exp(score[k, part, :] - top)
            score[k, part, :] = e
            w = e * dprob[k, part, :]
            total = e if k == 0 else total + e
            dots = w if k == 0 else dots + w
        inv = 1.0 / jnp.sum(total, axis=1, keepdims=True)
        row_dot = jnp.sum(dots, axis=1, keepdims=True) * inv
        for k in range(BACK):
            prob = score[k, part, :] * inv
            grad = prob * (dprob[k, part, :] - row_dot) * score_scale
            mixed[k, part, :] = grad.astype(jnp.bfloat16)
            mixed[k, QH + i * HEADS : QH + (i + 1) * HEADS, :] = prob.astype(jnp.bfloat16)

    blank = jnp.zeros((ROWS - KW, PAIR), jnp.bfloat16)
    for slot in range(2):
        keep_ref[slot, KW:, :] = blank
        send_ref[slot, KW:, :] = blank
    mid_ref[KW:, :] = (keys[2, KW:ROWS, :].astype(jnp.float32) * 0.5).astype(jnp.bfloat16)

    def grads(k):
        g = jnp.dot(cols_ref[...], mixed[k], preferred_element_type=jnp.float32)
        return g.astype(jnp.bfloat16)

    for slot in range(2):
        send_ref[slot, :KW, :] = grads(jnp.where(core == 0, 4 - slot, slot))
    for slot in range(2):
        keep_ref[slot, :KW, :] = grads(jnp.where(core == 0, slot, 4 - slot))
    mid_ref[:KW, :] = grads(2)


def vmem():
    return pl.BlockSpec(memory_space=pltpu.VMEM)


def smem():
    return pl.BlockSpec(memory_space=pltpu.SMEM)


def attention(info, own, par, rows, cols):
    block = jax.ShapeDtypeStruct((2, ROWS, PAIR), jnp.bfloat16)
    return pl.pallas_call(
        attention_kernel,
        out_shape=(block, block, jax.ShapeDtypeStruct((ROWS, PAIR), jnp.bfloat16)),
        in_specs=[smem()] + [vmem()] * 4,
        out_specs=(vmem(), vmem(), vmem()),
        scratch_shapes=[
            pltpu.VMEM((BACK, ROWS, PAIR), jnp.bfloat16),
            pltpu.VMEM((BACK, QH, PAIR), jnp.float32),
            pltpu.VMEM((BACK, QH, PAIR), jnp.float32),
            pltpu.VMEM((BACK, 2 * QH, PAIR), jnp.bfloat16),
        ],
        compiler_params=pltpu.CompilerParams(vmem_limit_bytes=24 * MIB),
        name="attention_grads",
    )(info, own, par, rows, cols)


def down_kernel(
    info, limits, g0, r12, r34, s12, s34, hidden, out_ref, own_ref, last, scaled, weight,
):
    chip, core = info[0], info[1]
    mine = pl.ds(pl.multiple_of(core * TOK, TOK), TOK)
    other = pl.ds(pl.multiple_of((1 - core) * TOK, TOK), TOK)
    last[:, mine] = r34[:, PAIR:]
    last[:, other] = s34[:, PAIR:]

    @pl.when(core == 0)
    def _():
        own_ref[...] = s12[1, :KW, :TOK]

    @pl.when(core != 0)
    def _():
        own_ref[...] = r12[1, :KW, TOK:]

    away = jnp.where(core == 0, -1, 1)
    blocks = [(g0, 0), (r12.at[0], away), (r12.at[1], 2 * away), (r34.at[:, :PAIR], 3 * away)]
    blocks += [(s12.at[0], -away), (s12.at[1], -2 * away), (s34.at[:, :PAIR], -3 * away)]
    blocks += [(last, 4)]
    doc = lax.broadcasted_iota(jnp.int32, (NDOC, PAIR), 0).astype(jnp.float32)
    squares = jnp.zeros((NDOC, PAIR), jnp.float32)
    members = []
    for ref, _ in blocks:
        x = ref[:KW, :].astype(jnp.float32)
        ids = ref[KW:ROWS, :].astype(jnp.float32)[0:1]
        member = doc == ids
        members.append(member)
        squares = squares + jnp.where(member, jnp.sum(x * x, axis=0, keepdims=True), 0.0)
    norms = jnp.sum(squares, axis=1, keepdims=True)
    row = lax.broadcasted_iota(jnp.int32, (NDOC, NDOC), 0)
    col = lax.broadcasted_iota(jnp.int32, (NDOC, NDOC), 1)
    limit = jnp.sum(jnp.where(row == col, limits[...], 0.0), axis=1, keepdims=True)
    factor = jnp.minimum(1.0, limit / jnp.sqrt(norms + norm_eps))
    for (ref, by), member in zip(blocks, members, strict=True):
        gain = jnp.sum(jnp.where(member, factor, 0.0), axis=0, keepdims=True)
        shard = lax.rem(chip + by + 2 * CHIPS - 2, CHIPS)
        x = ref[:KW, :].astype(jnp.float32) * gain
        scaled[:, pl.ds(pl.multiple_of(shard * PAIR, PAIR), PAIR)] = x.astype(jnp.bfloat16)
    product = lax.dot_general(
        scaled[...], hidden[...], (((1,), (1,)), ((), ())), preferred_element_type=jnp.float32
    )
    width = product.shape[1]
    weight[...] = jnp.zeros_like(weight)
    weight[:, :width] = product.astype(jnp.bfloat16)
    whole = weight[...]
    row = lax.broadcasted_iota(jnp.int32, (SLOT, KW), 0)
    col = lax.broadcasted_iota(jnp.int32, (SLOT, KW), 1)
    pick = (col == row + lax.shift_right_logical(row, 3)).astype(jnp.bfloat16)
    first = jnp.dot(pick, whole, preferred_element_type=jnp.float32)
    row = lax.broadcasted_iota(jnp.int32, (SLOT // 8, KW), 0)
    col = lax.broadcasted_iota(jnp.int32, (SLOT // 8, KW), 1)
    pick = (col == row * GRP_ROWS + 8).astype(jnp.bfloat16)
    ninth = jnp.dot(pick, whole, preferred_element_type=jnp.float32).astype(jnp.bfloat16)
    row = lax.broadcasted_iota(jnp.int32, (SLOT, 128), 0)
    col = lax.broadcasted_iota(jnp.int32, (SLOT, 128), 1)
    pieces = []
    for s in range(8):
        pick = ((row == col - 64 + s * TAIL) & (col >= 64) & (col < 64 + TAIL)).astype(jnp.bfloat16)
        pieces.append(
            jnp.dot(ninth, pick, preferred_element_type=jnp.float32).astype(jnp.bfloat16)
        )
    pieces = jnp.concatenate(pieces, axis=0)
    row = lax.broadcasted_iota(jnp.int32, (SLOT, SLOT), 0)
    col = lax.broadcasted_iota(jnp.int32, (SLOT, SLOT), 1)
    pick = (col == (row & 7) * 64 + lax.shift_right_logical(row, 3)).astype(jnp.bfloat16)
    tail = jnp.dot(pick, pieces, preferred_element_type=jnp.float32)
    out_ref[:, :384] = first[:, :384].astype(jnp.bfloat16)
    out_ref[:, 384:] = (first[:, 384:] + tail).astype(jnp.bfloat16)


def down_grad(info, limits, blocks, hidden):
    return pl.pallas_call(
        down_kernel,
        out_shape=(
            jax.ShapeDtypeStruct((SLOT, SLOT), jnp.bfloat16),
            jax.ShapeDtypeStruct((KW, TOK), jnp.bfloat16),
        ),
        in_specs=[smem()] + [vmem()] * 7,
        out_specs=(vmem(), vmem()),
        scratch_shapes=[
            pltpu.VMEM((ROWS, PAIR), jnp.bfloat16),
            pltpu.VMEM((KW, CHIPS * PAIR), jnp.bfloat16),
            pltpu.VMEM((KW, SLOT), jnp.bfloat16),
        ],
        compiler_params=pltpu.CompilerParams(vmem_limit_bytes=20 * MIB),
        name="down_grad",
    )(info, limits, *blocks, hidden)


def added(*terms):
    total = terms[0].astype(jnp.float32)
    for term in terms[1:]:
        total = total + term.astype(jnp.float32)
    return total.astype(jnp.bfloat16)


def group_part(latent, queries, out_grad, hidden, doc_ids, clip_limits):
    position = lax.axis_index("ctx")
    core = position % 2
    info = jnp.stack([position // 2, core]).astype(jnp.int32)
    ids = jnp.pad(doc_ids.astype(jnp.bfloat16), ((0, ROWS - KW - 1), (0, 0)))
    keys = jnp.concatenate([latent[0].T, ids], axis=0)
    near = chip_shift(keys, 1, 1)
    fourth = chip_shift(keys, 4, 4)
    next_near = chip_shift(keys, 2, 2)
    next_near, query_rows, grad_rows = lax.optimization_barrier((next_near, queries, out_grad))
    query_rows = query_rows[0].reshape(QH, KW)
    grad_rows = grad_rows[0].reshape(QH, LATENT)
    rows = jnp.concatenate([query_rows, jnp.pad(grad_rows, ((0, 0), (0, KW - LATENT)))], axis=0)
    cols = rows.T
    own = jnp.stack([keys, near, next_near, chip_shift(near, 2, 2), fourth])
    own, rows, cols, info = lax.optimization_barrier((own, rows, cols, info))
    par = core_swap(own)
    keep, send, mid = attention(info, own, par, rows, cols)

    arrived = core_swap(send)
    far = chip_shift(added(keep[0], arrived[0]), 2, -2)
    close = chip_shift(added(keep[1], arrived[1]), 1, -1)
    mine = added(mid, far, close)
    total = added(mine, core_swap(mine))

    one = chip_shift(total, 1, -1)
    two = chip_shift(total, 2, -2)
    three = chip_shift(one, 2, -2)
    half = jnp.where(core == 0, two[:, :TOK], two[:, TOK:])
    four = chip_shift(half, 2, -2)
    one, two, three = lax.optimization_barrier((one, two, three))
    nearer = jnp.stack([one, two])
    nearer_par = core_swap(nearer)
    farther = jnp.concatenate([three, four], axis=1)
    blocks = [total, nearer, farther, nearer_par, core_swap(farther)]
    chunks, own_grad = down_grad(info, clip_limits, blocks, hidden[0].T)
    return own_grad, chunks


def on_device(latent, queries, out_grad, hidden, doc_ids, clip_limits):
    own_grad, chunks = group_part(latent, queries, out_grad, hidden, doc_ids, clip_limits)
    groups = lax.axis_size("grp")
    chunks = chunks.reshape(groups, SLOT // groups, SLOT)
    chunks = lax.all_to_all(chunks, "grp", 0, 0, tiled=True)
    mine = jnp.sum(chunks.astype(jnp.float32), axis=0)
    width = hidden.shape[2]
    ninth = mine[:, width : width + TAIL].reshape(1, width)
    weight_grad = jnp.concatenate([mine[:, :width], ninth], axis=0)
    return own_grad.T[None], weight_grad


def solution(mesh):
    return jax.shard_map(
        on_device,
        mesh=mesh,
        in_specs=(
            P("grp", "ctx", None),
            P("grp", "ctx", None),
            P("grp", "ctx", None),
            P("grp", None, "ctx"),
            P("grp", "ctx"),
            P("grp", None),
        ),
        out_specs=(P("grp", "ctx", None), P("grp", "ctx")),
        check_vma=False,
    )
```

```python
import functools

import jax
import jax.numpy as jnp
from jax import lax
from jax.experimental import pallas as pl
from jax.experimental.pallas import tpu as pltpu
from jax.sharding import PartitionSpec as P

LATENT = 512
KW = 576
HEADS = 128
TOK = 128
Q_DEV = 4
NDOC = 8
CHIPS = 8
BACK = 5
ROWS = 592
PAIR = 2 * TOK
QH = Q_DEV * HEADS
SLOT = 512
GRP_ROWS = 9
TAIL = 56

score_scale = 192.0 ** (-0.5)
norm_eps = 1e-06
MIB = 1024 * 1024


def chip_shift(value, by0, by1):
    pairs = []
    for chip in range(CHIPS):
        for core, by in ((0, by0), (1, by1)):
            if by is not None:
                pairs.append((2 * chip + core, 2 * ((chip + by) % CHIPS) + core))
    return lax.ppermute(value, "ctx", pairs)


def core_swap(value):
    return lax.ppermute(value, "ctx", [(i, i ^ 1) for i in range(2 * CHIPS)])


def pack_kernel(latent_ref, ids_ref, out_ref):
    out_ref[:KW, :] = latent_ref[...]
    ids = jnp.broadcast_to(ids_ref[...].astype(jnp.float32), (ROWS - KW, TOK))
    out_ref[KW:, :] = ids.astype(jnp.bfloat16)


def rows_kernel(query_ref, grad_ref, rows_ref, cols_ref):
    rows_ref[:QH, :] = query_ref[...]
    rows_ref[QH:, :LATENT] = grad_ref[...]
    rows_ref[QH:, LATENT:] = jnp.zeros((QH, KW - LATENT), jnp.bfloat16)
    cols_ref[:, :QH] = query_ref[...].T
    cols_ref[:LATENT, QH:] = grad_ref[...].T
    cols_ref[LATENT:, QH:] = jnp.zeros((KW - LATENT, QH), jnp.bfloat16)


def block_dots(rows_ref, blocks, out_ref):
    for k in range(0, BACK - 1, 2):
        two = jnp.concatenate([blocks[k, :KW, :], blocks[k + 1, :KW, :]], axis=1)
        both = jnp.dot(rows_ref[...], two, preferred_element_type=jnp.float32)
        out_ref[k] = both[:, :TOK]
        out_ref[k + 1] = both[:, TOK:]
    out_ref[BACK - 1] = jnp.dot(
        rows_ref[...], blocks[BACK - 1, :KW, :], preferred_element_type=jnp.float32
    )


def scores_kernel(own, rows_ref, out_ref):
    block_dots(rows_ref, own, out_ref)


def grads_of(cols_ref, mixed, k):
    g = jnp.dot(cols_ref[...], mixed[k], preferred_element_type=jnp.float32)
    return g.astype(jnp.bfloat16)


def lanes_of(core):
    mine = pl.ds(pl.multiple_of(core * TOK, TOK), TOK)
    other = pl.ds(pl.multiple_of((1 - core) * TOK, TOK), TOK)
    return mine, other


def attention_kernel(
    info, own, par, own_both, rows_ref, cols_ref, send_ref, mixed, par_both, score
):
    chip, core = info[0], info[1]
    block_dots(rows_ref, par, par_both)
    own_ids = own[0, KW:ROWS, :].astype(jnp.float32)[0:1]
    lane = lax.broadcasted_iota(jnp.int32, (1, TOK), 1)
    query_ids = [
        jnp.sum(jnp.where(lane == TOK - Q_DEV + i, own_ids, 0.0), axis=1, keepdims=True)
        for i in range(Q_DEV)
    ]
    both = (own_both, par_both)
    tops = [None] * Q_DEV
    for k in range(BACK):
        there = chip - k >= 0
        for side, keys in enumerate((own, par)):
            ids = keys[k, KW:ROWS, :].astype(jnp.float32)[0:1]
            place = lane - k * PAIR + (core if side == 0 else 1 - core) * TOK
            for i in range(Q_DEV):
                at = core * TOK + TOK - Q_DEV + i
                allowed = (ids == query_ids[i]) & (place <= at) & there
                part = slice(i * HEADS, (i + 1) * HEADS)
                s = jnp.where(allowed, both[side][k, part, :] * score_scale, -1e30)
                score[side, k, part, :] = s
                tops[i] = s if tops[i] is None else jnp.maximum(tops[i], s)
    for i in range(Q_DEV):
        part = slice(i * HEADS, (i + 1) * HEADS)
        low = slice(QH + i * HEADS, QH + (i + 1) * HEADS)
        top = jnp.max(tops[i], axis=1, keepdims=True)
        total = dots = None
        for k in range(BACK):
            for side in range(2):
                e = jnp.exp(score[side, k, part, :] - top)
                score[side, k, part, :] = e
                w = e * both[side][k, low, :]
                total = e if total is None else total + e
                dots = w if dots is None else dots + w
        inv = 1.0 / jnp.sum(total, axis=1, keepdims=True)
        row_dot = jnp.sum(dots, axis=1, keepdims=True) * inv
        for k in range(BACK):
            for side in range(2):
                prob = score[side, k, part, :] * inv
                grad = prob * (both[side][k, low, :] - row_dot) * score_scale
                span = slice(side * TOK, (side + 1) * TOK)
                mixed[k, part, span] = grad.astype(jnp.bfloat16)
                mixed[k, low, span] = prob.astype(jnp.bfloat16)

    mine, other = lanes_of(core)
    for slot in range(2):
        g = grads_of(cols_ref, mixed, jnp.where(core == 0, 4 - slot, slot))
        send_ref[slot, :KW, mine] = g[:, :TOK]
        send_ref[slot, :KW, other] = g[:, TOK:]
        send_ref[slot, KW:, :] = jnp.zeros((ROWS - KW, PAIR), jnp.bfloat16)


def kept_kernel(info, own, par, mixed, cols_ref, keep_ref, mid_ref):
    core = info[1]
    mine, other = lanes_of(core)
    for slot in range(2):
        g = grads_of(cols_ref, mixed, jnp.where(core == 0, slot, 4 - slot))
        keep_ref[slot, :KW, mine] = g[:, :TOK]
        keep_ref[slot, :KW, other] = g[:, TOK:]
        keep_ref[slot, KW:, :] = jnp.zeros((ROWS - KW, PAIR), jnp.bfloat16)
    g = grads_of(cols_ref, mixed, 2)
    mid_ref[:KW, mine] = g[:, :TOK]
    mid_ref[:KW, other] = g[:, TOK:]
    for side, where in ((own, mine), (par, other)):
        half = side[2, KW:ROWS, :].astype(jnp.float32) * 0.5
        mid_ref[KW:, where] = half.astype(jnp.bfloat16)


def vmem():
    return pl.BlockSpec(memory_space=pltpu.VMEM)


def smem():
    return pl.BlockSpec(memory_space=pltpu.SMEM)


def call(kernel, shapes, smem_first, count, mib, scratch, flops, name, operands):
    specs = [smem()] * smem_first + [vmem()] * count
    return pl.pallas_call(
        kernel,
        out_shape=shapes,
        in_specs=specs,
        out_specs=jax.tree.map(lambda _: vmem(), shapes),
        scratch_shapes=scratch,
        compiler_params=pltpu.CompilerParams(vmem_limit_bytes=mib * MIB),
        cost_estimate=pl.CostEstimate(flops=flops, bytes_accessed=4 * MIB, transcendentals=0),
        name=name,
    )(*operands)


def shape(dims, dtype=jnp.bfloat16):
    return jax.ShapeDtypeStruct(dims, dtype)


def pack(latent, ids):
    return call(pack_kernel, shape((ROWS, TOK)), 0, 2, 4, [], 0, "pack_keys", (latent, ids))


def query_views(queries, grads):
    shapes = (shape((2 * QH, KW)), shape((KW, 2 * QH)))
    return call(rows_kernel, shapes, 0, 2, 16, [], 0, "query_views", (queries, grads))


def scores_of(own, rows):
    out = shape((BACK, 2 * QH, TOK), jnp.float32)
    flops = 4 * QH * KW * BACK * TOK
    return call(scores_kernel, out, 0, 2, 20, [], flops, "own_scores", (own, rows))


def attention(info, own, par, own_both, rows, cols):
    shapes = (shape((2, ROWS, PAIR)), shape((BACK, 2 * QH, PAIR)))
    scratch = [
        pltpu.VMEM((BACK, 2 * QH, TOK), jnp.float32),
        pltpu.VMEM((2, BACK, QH, TOK), jnp.float32),
    ]
    operands = (info, own, par, own_both, rows, cols)
    flops = 8 * QH * KW * BACK * TOK
    return call(attention_kernel, shapes, 1, 5, 28, scratch, flops, "attention_grads", operands)


def kept(info, own, par, mixed, cols):
    shapes = (shape((2, ROWS, PAIR)), shape((ROWS, PAIR)))
    flops = 6 * 2 * QH * KW * PAIR
    return call(kept_kernel, shapes, 1, 4, 20, [], flops, "kept_grads", (info, own, par, mixed, cols))


def down_kernel(
    info, limits, g0, r12, r34, s12, s34, hidden, out_ref, own_ref, last, scaled, weight,
):
    chip, core = info[0], info[1]
    mine = pl.ds(pl.multiple_of(core * TOK, TOK), TOK)
    other = pl.ds(pl.multiple_of((1 - core) * TOK, TOK), TOK)
    last[:, mine] = r34[:, PAIR:]
    last[:, other] = s34[:, PAIR:]

    @pl.when(core == 0)
    def _():
        own_ref[...] = s12[1, :KW, :TOK]

    @pl.when(core != 0)
    def _():
        own_ref[...] = r12[1, :KW, TOK:]

    away = jnp.where(core == 0, -1, 1)
    blocks = [(g0, 0), (r12.at[0], away), (r12.at[1], 2 * away), (r34.at[:, :PAIR], 3 * away)]
    blocks += [(s12.at[0], -away), (s12.at[1], -2 * away), (s34.at[:, :PAIR], -3 * away)]
    blocks += [(last, 4)]
    doc = lax.broadcasted_iota(jnp.int32, (NDOC, PAIR), 0).astype(jnp.float32)
    squares = jnp.zeros((NDOC, PAIR), jnp.float32)
    members = []
    for ref, _ in blocks:
        x = ref[:KW, :].astype(jnp.float32)
        ids = ref[KW:ROWS, :].astype(jnp.float32)[0:1]
        member = doc == ids
        members.append(member)
        squares = squares + jnp.where(member, jnp.sum(x * x, axis=0, keepdims=True), 0.0)
    norms = jnp.sum(squares, axis=1, keepdims=True)
    row = lax.broadcasted_iota(jnp.int32, (NDOC, NDOC), 0)
    col = lax.broadcasted_iota(jnp.int32, (NDOC, NDOC), 1)
    limit = jnp.sum(jnp.where(row == col, limits[...], 0.0), axis=1, keepdims=True)
    factor = jnp.minimum(1.0, limit / jnp.sqrt(norms + norm_eps))
    for (ref, by), member in zip(blocks, members, strict=True):
        gain = jnp.sum(jnp.where(member, factor, 0.0), axis=0, keepdims=True)
        shard = lax.rem(chip + by + 2 * CHIPS - 2, CHIPS)
        x = ref[:KW, :].astype(jnp.float32) * gain
        scaled[:, pl.ds(pl.multiple_of(shard * PAIR, PAIR), PAIR)] = x.astype(jnp.bfloat16)
    product = lax.dot_general(
        scaled[...], hidden[...], (((1,), (1,)), ((), ())), preferred_element_type=jnp.float32
    )
    width = product.shape[1]
    weight[...] = jnp.zeros_like(weight)
    weight[:, :width] = product.astype(jnp.bfloat16)
    whole = weight[...]
    row = lax.broadcasted_iota(jnp.int32, (SLOT, KW), 0)
    col = lax.broadcasted_iota(jnp.int32, (SLOT, KW), 1)
    pick = (col == row + lax.shift_right_logical(row, 3)).astype(jnp.bfloat16)
    first = jnp.dot(pick, whole, preferred_element_type=jnp.float32)
    row = lax.broadcasted_iota(jnp.int32, (SLOT // 8, KW), 0)
    col = lax.broadcasted_iota(jnp.int32, (SLOT // 8, KW), 1)
    pick = (col == row * GRP_ROWS + 8).astype(jnp.bfloat16)
    ninth = jnp.dot(pick, whole, preferred_element_type=jnp.float32).astype(jnp.bfloat16)
    row = lax.broadcasted_iota(jnp.int32, (SLOT, 128), 0)
    col = lax.broadcasted_iota(jnp.int32, (SLOT, 128), 1)
    pieces = []
    for s in range(8):
        pick = ((row == col - 64 + s * TAIL) & (col >= 64) & (col < 64 + TAIL)).astype(jnp.bfloat16)
        pieces.append(
            jnp.dot(ninth, pick, preferred_element_type=jnp.float32).astype(jnp.bfloat16)
        )
    pieces = jnp.concatenate(pieces, axis=0)
    row = lax.broadcasted_iota(jnp.int32, (SLOT, SLOT), 0)
    col = lax.broadcasted_iota(jnp.int32, (SLOT, SLOT), 1)
    pick = (col == (row & 7) * 64 + lax.shift_right_logical(row, 3)).astype(jnp.bfloat16)
    tail = jnp.dot(pick, pieces, preferred_element_type=jnp.float32)
    out_ref[:, :384] = first[:, :384].astype(jnp.bfloat16)
    out_ref[:, 384:] = (first[:, 384:] + tail).astype(jnp.bfloat16)


def down_grad(info, limits, blocks, hidden):
    return pl.pallas_call(
        down_kernel,
        out_shape=(
            jax.ShapeDtypeStruct((SLOT, SLOT), jnp.bfloat16),
            jax.ShapeDtypeStruct((KW, TOK), jnp.bfloat16),
        ),
        in_specs=[smem()] + [vmem()] * 7,
        out_specs=(vmem(), vmem()),
        scratch_shapes=[
            pltpu.VMEM((ROWS, PAIR), jnp.bfloat16),
            pltpu.VMEM((KW, CHIPS * PAIR), jnp.bfloat16),
            pltpu.VMEM((KW, SLOT), jnp.bfloat16),
        ],
        compiler_params=pltpu.CompilerParams(vmem_limit_bytes=20 * MIB),
        name="down_grad",
    )(info, limits, *blocks, hidden)


def added(*terms):
    total = terms[0].astype(jnp.float32)
    for term in terms[1:]:
        total = total + term.astype(jnp.float32)
    return total.astype(jnp.bfloat16)


def group_part(latent, queries, out_grad, hidden, doc_ids, clip_limits):
    position = lax.axis_index("ctx")
    core = position % 2
    info = jnp.stack([position // 2, core]).astype(jnp.int32)
    keys = pack(latent[0].T, doc_ids)
    near = chip_shift(keys, 1, 1)
    next_near = chip_shift(keys, 2, 2)
    query_rows = queries[0].reshape(QH, KW)
    far_keys, query_rows = lax.optimization_barrier((keys, query_rows))
    fourth = chip_shift(far_keys, 4, 4)
    near, grads = lax.optimization_barrier((near, out_grad))
    grad_rows = grads[0].reshape(QH, LATENT)
    rows, cols = query_views(query_rows, grad_rows)
    third = chip_shift(near, 2, 2)
    own = jnp.stack([keys, near, next_near, third, fourth])
    own, rows, cols, info = lax.optimization_barrier((own, rows, cols, info))
    par = core_swap(own)
    send, mixed = attention(info, own, par, scores_of(own, rows), rows, cols)
    keep, mid = kept(info, own, par, mixed, cols)

    arrived = core_swap(send)
    far = chip_shift(added(keep[0], arrived[0]), 2, -2)
    close = chip_shift(added(keep[1], arrived[1]), 1, -1)
    mine = added(mid, far, close)
    total = added(mine, core_swap(mine))

    one = chip_shift(total, 1, -1)
    two = chip_shift(total, 2, -2)
    three = chip_shift(one, 2, -2)
    half = jnp.where(core == 0, two[:, :TOK], two[:, TOK:])
    four = chip_shift(half, 2, -2)
    one, two, three = lax.optimization_barrier((one, two, three))
    nearer = jnp.stack([one, two])
    nearer_par = core_swap(nearer)
    farther = jnp.concatenate([three, four], axis=1)
    blocks = [total, nearer, farther, nearer_par, core_swap(farther)]
    chunks, own_grad = down_grad(info, clip_limits, blocks, hidden[0].T)
    return own_grad, chunks


def on_device(latent, queries, out_grad, hidden, doc_ids, clip_limits):
    own_grad, chunks = group_part(latent, queries, out_grad, hidden, doc_ids, clip_limits)
    groups = lax.axis_size("grp")
    chunks = chunks.reshape(groups, SLOT // groups, SLOT)
    chunks = lax.all_to_all(chunks, "grp", 0, 0, tiled=True)
    mine = jnp.sum(chunks.astype(jnp.float32), axis=0)
    width = hidden.shape[2]
    ninth = mine[:, width : width + TAIL].reshape(1, width)
    weight_grad = jnp.concatenate([mine[:, :width], ninth], axis=0)
    return own_grad.T[None], weight_grad


def solution(mesh):
    return jax.shard_map(
        on_device,
        mesh=mesh,
        in_specs=(
            P("grp", "ctx", None),
            P("grp", "ctx", None),
            P("grp", "ctx", None),
            P("grp", None, "ctx"),
            P("grp", "ctx"),
            P("grp", None),
        ),
        out_specs=(P("grp", "ctx", None), P("grp", "ctx")),
        check_vma=False,
    )
```

```python
import functools

import jax
import jax.numpy as jnp
from jax import lax
from jax.experimental import pallas as pl
from jax.experimental.pallas import tpu as pltpu
from jax.sharding import PartitionSpec as P

LATENT = 512
KW = 576
HEADS = 128
TOK = 128
Q_DEV = 4
NDOC = 8
CHIPS = 8
BACK = 5
ROWS = 592
PAIR = 2 * TOK
QH = Q_DEV * HEADS
SLOT = 512
GRP_ROWS = 9
TAIL = 56

score_scale = 192.0 ** (-0.5)
norm_eps = 1e-06
MIB = 1024 * 1024


def chip_shift(value, by0, by1):
    pairs = []
    for chip in range(CHIPS):
        for core, by in ((0, by0), (1, by1)):
            if by is not None:
                pairs.append((2 * chip + core, 2 * ((chip + by) % CHIPS) + core))
    return lax.ppermute(value, "ctx", pairs)


def core_swap(value):
    return lax.ppermute(value, "ctx", [(i, i ^ 1) for i in range(2 * CHIPS)])


def pack_kernel(latent_ref, ids_ref, out_ref):
    out_ref[:KW, :] = latent_ref[...]
    ids = jnp.broadcast_to(ids_ref[...].astype(jnp.float32), (ROWS - KW, TOK))
    out_ref[KW:, :] = ids.astype(jnp.bfloat16)


def rows_kernel(query_ref, grad_ref, rows_ref, cols_ref):
    rows_ref[:QH, :] = query_ref[...]
    rows_ref[QH:, :LATENT] = grad_ref[...]
    rows_ref[QH:, LATENT:] = jnp.zeros((QH, KW - LATENT), jnp.bfloat16)
    cols_ref[:, :QH] = query_ref[...].T
    cols_ref[:LATENT, QH:] = grad_ref[...].T
    cols_ref[LATENT:, QH:] = jnp.zeros((KW - LATENT, QH), jnp.bfloat16)


def block_dots(rows_ref, blocks, out_ref):
    for k in range(0, BACK - 1, 2):
        two = jnp.concatenate([blocks[k, :KW, :], blocks[k + 1, :KW, :]], axis=1)
        both = jnp.dot(rows_ref[...], two, preferred_element_type=jnp.float32)
        out_ref[k] = both[:, :TOK]
        out_ref[k + 1] = both[:, TOK:]
    out_ref[BACK - 1] = jnp.dot(
        rows_ref[...], blocks[BACK - 1, :KW, :], preferred_element_type=jnp.float32
    )


def scores_kernel(own, rows_ref, out_ref):
    block_dots(rows_ref, own, out_ref)


def grads_of(cols_ref, mixed, k):
    g = jnp.dot(cols_ref[...], mixed[k], preferred_element_type=jnp.float32)
    return g.astype(jnp.bfloat16)


def lanes_of(core):
    mine = pl.ds(pl.multiple_of(core * TOK, TOK), TOK)
    other = pl.ds(pl.multiple_of((1 - core) * TOK, TOK), TOK)
    return mine, other


def attention_kernel(
    info, own, par, own_both, rows_ref, cols_ref, send_ref, mixed, par_both, score
):
    chip, core = info[0], info[1]
    block_dots(rows_ref, par, par_both)
    own_ids = own[0, KW:ROWS, :].astype(jnp.float32)[0:1]
    lane = lax.broadcasted_iota(jnp.int32, (1, TOK), 1)
    query_ids = [
        jnp.sum(jnp.where(lane == TOK - Q_DEV + i, own_ids, 0.0), axis=1, keepdims=True)
        for i in range(Q_DEV)
    ]
    both = (own_both, par_both)
    tops = [None] * Q_DEV
    for k in range(BACK):
        there = chip - k >= 0
        for side, keys in enumerate((own, par)):
            ids = keys[k, KW:ROWS, :].astype(jnp.float32)[0:1]
            place = lane - k * PAIR + (core if side == 0 else 1 - core) * TOK
            for i in range(Q_DEV):
                at = core * TOK + TOK - Q_DEV + i
                allowed = (ids == query_ids[i]) & (place <= at) & there
                part = slice(i * HEADS, (i + 1) * HEADS)
                s = jnp.where(allowed, both[side][k, part, :] * score_scale, -1e30)
                score[side, k, part, :] = s
                tops[i] = s if tops[i] is None else jnp.maximum(tops[i], s)
    for i in range(Q_DEV):
        part = slice(i * HEADS, (i + 1) * HEADS)
        low = slice(QH + i * HEADS, QH + (i + 1) * HEADS)
        top = jnp.max(tops[i], axis=1, keepdims=True)
        total = dots = None
        for k in range(BACK):
            for side in range(2):
                e = jnp.exp(score[side, k, part, :] - top)
                score[side, k, part, :] = e
                w = e * both[side][k, low, :]
                total = e if total is None else total + e
                dots = w if dots is None else dots + w
        inv = 1.0 / jnp.sum(total, axis=1, keepdims=True)
        row_dot = jnp.sum(dots, axis=1, keepdims=True) * inv
        for k in range(BACK):
            for side in range(2):
                prob = score[side, k, part, :] * inv
                grad = prob * (both[side][k, low, :] - row_dot) * score_scale
                span = slice(side * TOK, (side + 1) * TOK)
                mixed[k, part, span] = grad.astype(jnp.bfloat16)
                mixed[k, low, span] = prob.astype(jnp.bfloat16)

    mine, other = lanes_of(core)
    for slot in range(2):
        g = grads_of(cols_ref, mixed, jnp.where(core == 0, 4 - slot, slot))
        send_ref[slot, :KW, mine] = g[:, :TOK]
        send_ref[slot, :KW, other] = g[:, TOK:]
        send_ref[slot, KW:, :] = jnp.zeros((ROWS - KW, PAIR), jnp.bfloat16)


def kept_kernel(info, own, par, mixed, cols_ref, keep_ref, mid_ref):
    core = info[1]
    mine, other = lanes_of(core)
    for slot in range(2):
        g = grads_of(cols_ref, mixed, jnp.where(core == 0, slot, 4 - slot))
        keep_ref[slot, :KW, mine] = g[:, :TOK]
        keep_ref[slot, :KW, other] = g[:, TOK:]
        keep_ref[slot, KW:, :] = jnp.zeros((ROWS - KW, PAIR), jnp.bfloat16)
    g = grads_of(cols_ref, mixed, 2)
    mid_ref[:KW, mine] = g[:, :TOK]
    mid_ref[:KW, other] = g[:, TOK:]
    for side, where in ((own, mine), (par, other)):
        half = side[2, KW:ROWS, :].astype(jnp.float32) * 0.5
        mid_ref[KW:, where] = half.astype(jnp.bfloat16)


def vmem():
    return pl.BlockSpec(memory_space=pltpu.VMEM)


def smem():
    return pl.BlockSpec(memory_space=pltpu.SMEM)


def call(kernel, shapes, smem_first, count, mib, scratch, flops, name, operands):
    specs = [smem()] * smem_first + [vmem()] * count
    return pl.pallas_call(
        kernel,
        out_shape=shapes,
        in_specs=specs,
        out_specs=jax.tree.map(lambda _: vmem(), shapes),
        scratch_shapes=scratch,
        compiler_params=pltpu.CompilerParams(vmem_limit_bytes=mib * MIB),
        cost_estimate=pl.CostEstimate(flops=flops, bytes_accessed=4 * MIB, transcendentals=0),
        name=name,
    )(*operands)


def shape(dims, dtype=jnp.bfloat16):
    return jax.ShapeDtypeStruct(dims, dtype)


def pack(latent, ids):
    return call(pack_kernel, shape((ROWS, TOK)), 0, 2, 4, [], 0, "pack_keys", (latent, ids))


def query_views(queries, grads):
    shapes = (shape((2 * QH, KW)), shape((KW, 2 * QH)))
    return call(rows_kernel, shapes, 0, 2, 16, [], 0, "query_views", (queries, grads))


def scores_of(own, rows):
    out = shape((BACK, 2 * QH, TOK), jnp.float32)
    flops = 4 * QH * KW * BACK * TOK
    return call(scores_kernel, out, 0, 2, 20, [], flops, "own_scores", (own, rows))


def attention(info, own, par, own_both, rows, cols):
    shapes = (shape((2, ROWS, PAIR)), shape((BACK, 2 * QH, PAIR)))
    scratch = [
        pltpu.VMEM((BACK, 2 * QH, TOK), jnp.float32),
        pltpu.VMEM((2, BACK, QH, TOK), jnp.float32),
    ]
    operands = (info, own, par, own_both, rows, cols)
    flops = 8 * QH * KW * BACK * TOK
    return call(attention_kernel, shapes, 1, 5, 28, scratch, flops, "attention_grads", operands)


def kept(info, own, par, mixed, cols):
    shapes = (shape((2, ROWS, PAIR)), shape((ROWS, PAIR)))
    flops = 6 * 2 * QH * KW * PAIR
    return call(kept_kernel, shapes, 1, 4, 20, [], flops, "kept_grads", (info, own, par, mixed, cols))


def down_kernel(
    info, limits, g0, r12, r34, s12, s34, hidden, out_ref, own_ref, last, scaled, weight,
):
    chip, core = info[0], info[1]
    mine = pl.ds(pl.multiple_of(core * TOK, TOK), TOK)
    other = pl.ds(pl.multiple_of((1 - core) * TOK, TOK), TOK)
    last[:, mine] = r34[:, PAIR:]
    last[:, other] = s34[:, PAIR:]

    @pl.when(core == 0)
    def _():
        own_ref[...] = s12[1, :KW, :TOK]

    @pl.when(core != 0)
    def _():
        own_ref[...] = r12[1, :KW, TOK:]

    away = jnp.where(core == 0, -1, 1)
    blocks = [(g0, 0), (r12.at[0], away), (r12.at[1], 2 * away), (r34.at[:, :PAIR], 3 * away)]
    blocks += [(s12.at[0], -away), (s12.at[1], -2 * away), (s34.at[:, :PAIR], -3 * away)]
    blocks += [(last, 4)]
    doc = lax.broadcasted_iota(jnp.int32, (NDOC, PAIR), 0).astype(jnp.float32)
    squares = jnp.zeros((NDOC, PAIR), jnp.float32)
    members = []
    for ref, _ in blocks:
        x = ref[:KW, :].astype(jnp.float32)
        ids = ref[KW:ROWS, :].astype(jnp.float32)[0:1]
        member = doc == ids
        members.append(member)
        squares = squares + jnp.where(member, jnp.sum(x * x, axis=0, keepdims=True), 0.0)
    norms = jnp.sum(squares, axis=1, keepdims=True)
    row = lax.broadcasted_iota(jnp.int32, (NDOC, NDOC), 0)
    col = lax.broadcasted_iota(jnp.int32, (NDOC, NDOC), 1)
    limit = jnp.sum(jnp.where(row == col, limits[...], 0.0), axis=1, keepdims=True)
    factor = jnp.minimum(1.0, limit / jnp.sqrt(norms + norm_eps))
    for (ref, by), member in zip(blocks, members, strict=True):
        gain = jnp.sum(jnp.where(member, factor, 0.0), axis=0, keepdims=True)
        shard = lax.rem(chip + by + 2 * CHIPS - 2, CHIPS)
        x = ref[:KW, :].astype(jnp.float32) * gain
        scaled[:, pl.ds(pl.multiple_of(shard * PAIR, PAIR), PAIR)] = x.astype(jnp.bfloat16)
    product = lax.dot_general(
        scaled[...], hidden[...], (((1,), (1,)), ((), ())), preferred_element_type=jnp.float32
    )
    width = product.shape[1]
    weight[...] = jnp.zeros_like(weight)
    weight[:, :width] = product.astype(jnp.bfloat16)
    whole = weight[...]
    row = lax.broadcasted_iota(jnp.int32, (SLOT, KW), 0)
    col = lax.broadcasted_iota(jnp.int32, (SLOT, KW), 1)
    pick = (col == row + lax.shift_right_logical(row, 3)).astype(jnp.bfloat16)
    first = jnp.dot(pick, whole, preferred_element_type=jnp.float32)
    row = lax.broadcasted_iota(jnp.int32, (SLOT // 8, KW), 0)
    col = lax.broadcasted_iota(jnp.int32, (SLOT // 8, KW), 1)
    pick = (col == row * GRP_ROWS + 8).astype(jnp.bfloat16)
    ninth = jnp.dot(pick, whole, preferred_element_type=jnp.float32).astype(jnp.bfloat16)
    row = lax.broadcasted_iota(jnp.int32, (SLOT, 128), 0)
    col = lax.broadcasted_iota(jnp.int32, (SLOT, 128), 1)
    pieces = []
    for s in range(8):
        pick = ((row == col - 64 + s * TAIL) & (col >= 64) & (col < 64 + TAIL)).astype(jnp.bfloat16)
        pieces.append(
            jnp.dot(ninth, pick, preferred_element_type=jnp.float32).astype(jnp.bfloat16)
        )
    pieces = jnp.concatenate(pieces, axis=0)
    row = lax.broadcasted_iota(jnp.int32, (SLOT, SLOT), 0)
    col = lax.broadcasted_iota(jnp.int32, (SLOT, SLOT), 1)
    pick = (col == (row & 7) * 64 + lax.shift_right_logical(row, 3)).astype(jnp.bfloat16)
    tail = jnp.dot(pick, pieces, preferred_element_type=jnp.float32)
    out_ref[:, :384] = first[:, :384].astype(jnp.bfloat16)
    out_ref[:, 384:] = (first[:, 384:] + tail).astype(jnp.bfloat16)


def down_grad(info, limits, blocks, hidden):
    return pl.pallas_call(
        down_kernel,
        out_shape=(
            jax.ShapeDtypeStruct((SLOT, SLOT), jnp.bfloat16),
            jax.ShapeDtypeStruct((KW, TOK), jnp.bfloat16),
        ),
        in_specs=[smem()] + [vmem()] * 7,
        out_specs=(vmem(), vmem()),
        scratch_shapes=[
            pltpu.VMEM((ROWS, PAIR), jnp.bfloat16),
            pltpu.VMEM((KW, CHIPS * PAIR), jnp.bfloat16),
            pltpu.VMEM((KW, SLOT), jnp.bfloat16),
        ],
        compiler_params=pltpu.CompilerParams(vmem_limit_bytes=20 * MIB),
        name="down_grad",
    )(info, limits, *blocks, hidden)


def added(*terms):
    total = terms[0].astype(jnp.float32)
    for term in terms[1:]:
        total = total + term.astype(jnp.float32)
    return total.astype(jnp.bfloat16)


def group_part(latent, queries, out_grad, hidden, doc_ids, clip_limits):
    position = lax.axis_index("ctx")
    core = position % 2
    info = jnp.stack([position // 2, core]).astype(jnp.int32)
    keys = pack(latent[0].T, doc_ids)
    near = chip_shift(keys, 1, 1)
    next_near = chip_shift(keys, 2, 2)
    query_rows = queries[0].reshape(QH, KW)
    far_keys, info = lax.optimization_barrier((keys, info))
    fourth = chip_shift(far_keys, 4, 4)
    near, grads = lax.optimization_barrier((near, out_grad))
    grad_rows = grads[0].reshape(QH, LATENT)
    rows, cols = query_views(query_rows, grad_rows)
    third = chip_shift(near, 2, 2)
    own = jnp.stack([keys, near, next_near, third, fourth])
    own, rows, cols, info = lax.optimization_barrier((own, rows, cols, info))
    par = core_swap(own)
    send, mixed = attention(info, own, par, scores_of(own, rows), rows, cols)
    keep, mid = kept(info, own, par, mixed, cols)

    arrived = core_swap(send)
    far = chip_shift(added(keep[0], arrived[0]), 2, -2)
    close = chip_shift(added(keep[1], arrived[1]), 1, -1)
    mine = added(mid, far, close)
    total = added(mine, core_swap(mine))

    one = chip_shift(total, 1, -1)
    two = chip_shift(total, 2, -2)
    three = chip_shift(one, 2, -2)
    half = jnp.where(core == 0, two[:, :TOK], two[:, TOK:])
    four = chip_shift(half, 2, -2)
    one, two, three = lax.optimization_barrier((one, two, three))
    nearer = jnp.stack([one, two])
    nearer_par = core_swap(nearer)
    farther = jnp.concatenate([three, four], axis=1)
    blocks = [total, nearer, farther, nearer_par, core_swap(farther)]
    chunks, own_grad = down_grad(info, clip_limits, blocks, hidden[0].T)
    return own_grad, chunks


def on_device(latent, queries, out_grad, hidden, doc_ids, clip_limits):
    own_grad, chunks = group_part(latent, queries, out_grad, hidden, doc_ids, clip_limits)
    groups = lax.axis_size("grp")
    chunks = chunks.reshape(groups, SLOT // groups, SLOT)
    chunks = lax.all_to_all(chunks, "grp", 0, 0, tiled=True)
    mine = jnp.sum(chunks.astype(jnp.float32), axis=0)
    width = hidden.shape[2]
    ninth = mine[:, width : width + TAIL].reshape(1, width)
    weight_grad = jnp.concatenate([mine[:, :width], ninth], axis=0)
    return own_grad.T[None], weight_grad


def solution(mesh):
    return jax.shard_map(
        on_device,
        mesh=mesh,
        in_specs=(
            P("grp", "ctx", None),
            P("grp", "ctx", None),
            P("grp", "ctx", None),
            P("grp", None, "ctx"),
            P("grp", "ctx"),
            P("grp", None),
        ),
        out_specs=(P("grp", "ctx", None), P("grp", "ctx")),
        check_vma=False,
    )
```

```python
import functools

import jax
import jax.numpy as jnp
from jax import lax
from jax.experimental import pallas as pl
from jax.experimental.pallas import tpu as pltpu
from jax.sharding import PartitionSpec as P

LATENT = 512
KW = 576
HEADS = 128
TOK = 128
Q_DEV = 4
NDOC = 8
CHIPS = 8
BACK = 5
ROWS = 592
PAIR = 2 * TOK
QH = Q_DEV * HEADS
SLOT = 512
GRP_ROWS = 9
TAIL = 56

score_scale = 192.0 ** (-0.5)
norm_eps = 1e-06
MIB = 1024 * 1024


def chip_shift(value, by0, by1):
    pairs = []
    for chip in range(CHIPS):
        for core, by in ((0, by0), (1, by1)):
            if by is not None:
                pairs.append((2 * chip + core, 2 * ((chip + by) % CHIPS) + core))
    return lax.ppermute(value, "ctx", pairs)


def core_swap(value):
    return lax.ppermute(value, "ctx", [(i, i ^ 1) for i in range(2 * CHIPS)])


def pack_kernel(latent_ref, ids_ref, out_ref):
    out_ref[:KW, :] = latent_ref[...]
    ids = jnp.broadcast_to(ids_ref[...].astype(jnp.float32), (ROWS - KW, TOK))
    out_ref[KW:, :] = ids.astype(jnp.bfloat16)


def rows_kernel(query_ref, grad_ref, rows_ref, cols_ref):
    rows_ref[:QH, :] = query_ref[...]
    rows_ref[QH:, :LATENT] = grad_ref[...]
    rows_ref[QH:, LATENT:] = jnp.zeros((QH, KW - LATENT), jnp.bfloat16)
    cols_ref[:, :QH] = query_ref[...].T
    cols_ref[:LATENT, QH:] = grad_ref[...].T
    cols_ref[LATENT:, QH:] = jnp.zeros((KW - LATENT, QH), jnp.bfloat16)


def block_dots(rows_ref, blocks, out_ref):
    for k in range(0, BACK - 1, 2):
        two = jnp.concatenate([blocks[k, :KW, :], blocks[k + 1, :KW, :]], axis=1)
        both = jnp.dot(rows_ref[...], two, preferred_element_type=jnp.float32)
        out_ref[k] = both[:, :TOK]
        out_ref[k + 1] = both[:, TOK:]
    out_ref[BACK - 1] = jnp.dot(
        rows_ref[...], blocks[BACK - 1, :KW, :], preferred_element_type=jnp.float32
    )


def scores_kernel(own, rows_ref, out_ref):
    block_dots(rows_ref, own, out_ref)


def grads_of(cols_ref, mixed, k):
    g = jnp.dot(cols_ref[...], mixed[k], preferred_element_type=jnp.float32)
    return g.astype(jnp.bfloat16)


def lanes_of(core):
    mine = pl.ds(pl.multiple_of(core * TOK, TOK), TOK)
    other = pl.ds(pl.multiple_of((1 - core) * TOK, TOK), TOK)
    return mine, other


def attention_kernel(
    info, own, par, own_both, rows_ref, cols_ref, send_ref, mixed, par_both, score
):
    chip, core = info[0], info[1]
    block_dots(rows_ref, par, par_both)
    own_ids = own[0, KW:ROWS, :].astype(jnp.float32)[0:1]
    lane = lax.broadcasted_iota(jnp.int32, (1, TOK), 1)
    query_ids = [
        jnp.sum(jnp.where(lane == TOK - Q_DEV + i, own_ids, 0.0), axis=1, keepdims=True)
        for i in range(Q_DEV)
    ]
    both = (own_both, par_both)
    tops = [None] * Q_DEV
    for k in range(BACK):
        there = chip - k >= 0
        for side, keys in enumerate((own, par)):
            ids = keys[k, KW:ROWS, :].astype(jnp.float32)[0:1]
            place = lane - k * PAIR + (core if side == 0 else 1 - core) * TOK
            for i in range(Q_DEV):
                at = core * TOK + TOK - Q_DEV + i
                allowed = (ids == query_ids[i]) & (place <= at) & there
                part = slice(i * HEADS, (i + 1) * HEADS)
                s = jnp.where(allowed, both[side][k, part, :] * score_scale, -1e30)
                score[side, k, part, :] = s
                tops[i] = s if tops[i] is None else jnp.maximum(tops[i], s)
    for i in range(Q_DEV):
        part = slice(i * HEADS, (i + 1) * HEADS)
        low = slice(QH + i * HEADS, QH + (i + 1) * HEADS)
        top = jnp.max(tops[i], axis=1, keepdims=True)
        total = dots = None
        for k in range(BACK):
            for side in range(2):
                e = jnp.exp(score[side, k, part, :] - top)
                score[side, k, part, :] = e
                w = e * both[side][k, low, :]
                total = e if total is None else total + e
                dots = w if dots is None else dots + w
        inv = 1.0 / jnp.sum(total, axis=1, keepdims=True)
        row_dot = jnp.sum(dots, axis=1, keepdims=True) * inv
        for k in range(BACK):
            for side in range(2):
                prob = score[side, k, part, :] * inv
                grad = prob * (both[side][k, low, :] - row_dot) * score_scale
                span = slice(side * TOK, (side + 1) * TOK)
                mixed[k, part, span] = grad.astype(jnp.bfloat16)
                mixed[k, low, span] = prob.astype(jnp.bfloat16)

    mine, other = lanes_of(core)
    for slot in range(2):
        g = grads_of(cols_ref, mixed, jnp.where(core == 0, 4 - slot, slot))
        send_ref[slot, :KW, mine] = g[:, :TOK]
        send_ref[slot, :KW, other] = g[:, TOK:]
        send_ref[slot, KW:, :] = jnp.zeros((ROWS - KW, PAIR), jnp.bfloat16)


def kept_kernel(info, own, par, mixed, cols_ref, keep_ref, mid_ref):
    core = info[1]
    mine, other = lanes_of(core)
    for slot in range(2):
        g = grads_of(cols_ref, mixed, jnp.where(core == 0, slot, 4 - slot))
        keep_ref[slot, :KW, mine] = g[:, :TOK]
        keep_ref[slot, :KW, other] = g[:, TOK:]
        keep_ref[slot, KW:, :] = jnp.zeros((ROWS - KW, PAIR), jnp.bfloat16)
    g = grads_of(cols_ref, mixed, 2)
    mid_ref[:KW, mine] = g[:, :TOK]
    mid_ref[:KW, other] = g[:, TOK:]
    for side, where in ((own, mine), (par, other)):
        half = side[2, KW:ROWS, :].astype(jnp.float32) * 0.5
        mid_ref[KW:, where] = half.astype(jnp.bfloat16)


def vmem():
    return pl.BlockSpec(memory_space=pltpu.VMEM)


def smem():
    return pl.BlockSpec(memory_space=pltpu.SMEM)


def call(kernel, shapes, smem_first, count, mib, scratch, flops, name, operands):
    specs = [smem()] * smem_first + [vmem()] * count
    return pl.pallas_call(
        kernel,
        out_shape=shapes,
        in_specs=specs,
        out_specs=jax.tree.map(lambda _: vmem(), shapes),
        scratch_shapes=scratch,
        compiler_params=pltpu.CompilerParams(vmem_limit_bytes=mib * MIB),
        cost_estimate=pl.CostEstimate(flops=flops, bytes_accessed=4 * MIB, transcendentals=0),
        name=name,
    )(*operands)


def shape(dims, dtype=jnp.bfloat16):
    return jax.ShapeDtypeStruct(dims, dtype)


def pack(latent, ids):
    return call(pack_kernel, shape((ROWS, TOK)), 0, 2, 4, [], 0, "pack_keys", (latent, ids))


def query_views(queries, grads):
    shapes = (shape((2 * QH, KW)), shape((KW, 2 * QH)))
    return call(rows_kernel, shapes, 0, 2, 16, [], 0, "query_views", (queries, grads))


def scores_of(own, rows):
    out = shape((BACK, 2 * QH, TOK), jnp.float32)
    flops = 4 * QH * KW * BACK * TOK
    return call(scores_kernel, out, 0, 2, 20, [], flops, "own_scores", (own, rows))


def attention(info, own, par, own_both, rows, cols):
    shapes = (shape((2, ROWS, PAIR)), shape((BACK, 2 * QH, PAIR)))
    scratch = [
        pltpu.VMEM((BACK, 2 * QH, TOK), jnp.float32),
        pltpu.VMEM((2, BACK, QH, TOK), jnp.float32),
    ]
    operands = (info, own, par, own_both, rows, cols)
    flops = 8 * QH * KW * BACK * TOK
    return call(attention_kernel, shapes, 1, 5, 28, scratch, flops, "attention_grads", operands)


def kept(info, own, par, mixed, cols):
    shapes = (shape((2, ROWS, PAIR)), shape((ROWS, PAIR)))
    flops = 6 * 2 * QH * KW * PAIR
    return call(kept_kernel, shapes, 1, 4, 20, [], flops, "kept_grads", (info, own, par, mixed, cols))


def down_kernel(
    info, limits, g0, r12, r34, s12, s34, hidden, out_ref, own_ref, last, scaled, weight,
):
    chip, core = info[0], info[1]
    mine = pl.ds(pl.multiple_of(core * TOK, TOK), TOK)
    other = pl.ds(pl.multiple_of((1 - core) * TOK, TOK), TOK)
    last[:, mine] = r34[:, PAIR:]
    last[:, other] = s34[:, PAIR:]

    @pl.when(core == 0)
    def _():
        own_ref[...] = s12[1, :KW, :TOK]

    @pl.when(core != 0)
    def _():
        own_ref[...] = r12[1, :KW, TOK:]

    away = jnp.where(core == 0, -1, 1)
    blocks = [(g0, 0), (r12.at[0], away), (r12.at[1], 2 * away), (r34.at[:, :PAIR], 3 * away)]
    blocks += [(s12.at[0], -away), (s12.at[1], -2 * away), (s34.at[:, :PAIR], -3 * away)]
    blocks += [(last, 4)]
    doc = lax.broadcasted_iota(jnp.int32, (NDOC, PAIR), 0).astype(jnp.float32)
    squares = jnp.zeros((NDOC, PAIR), jnp.float32)
    members = []
    for ref, _ in blocks:
        x = ref[:KW, :].astype(jnp.float32)
        ids = ref[KW:ROWS, :].astype(jnp.float32)[0:1]
        member = doc == ids
        members.append(member)
        squares = squares + jnp.where(member, jnp.sum(x * x, axis=0, keepdims=True), 0.0)
    norms = jnp.sum(squares, axis=1, keepdims=True)
    row = lax.broadcasted_iota(jnp.int32, (NDOC, NDOC), 0)
    col = lax.broadcasted_iota(jnp.int32, (NDOC, NDOC), 1)
    limit = jnp.sum(jnp.where(row == col, limits[...], 0.0), axis=1, keepdims=True)
    factor = jnp.minimum(1.0, limit / jnp.sqrt(norms + norm_eps))
    for (ref, by), member in zip(blocks, members, strict=True):
        gain = jnp.sum(jnp.where(member, factor, 0.0), axis=0, keepdims=True)
        shard = lax.rem(chip + by + 2 * CHIPS - 2, CHIPS)
        x = ref[:KW, :].astype(jnp.float32) * gain
        scaled[:, pl.ds(pl.multiple_of(shard * PAIR, PAIR), PAIR)] = x.astype(jnp.bfloat16)
    product = lax.dot_general(
        scaled[...], hidden[...], (((1,), (1,)), ((), ())), preferred_element_type=jnp.float32
    )
    width = product.shape[1]
    weight[...] = jnp.zeros_like(weight)
    weight[:, :width] = product.astype(jnp.bfloat16)
    whole = weight[...]
    row = lax.broadcasted_iota(jnp.int32, (SLOT, KW), 0)
    col = lax.broadcasted_iota(jnp.int32, (SLOT, KW), 1)
    pick = (col == row + lax.shift_right_logical(row, 3)).astype(jnp.bfloat16)
    first = jnp.dot(pick, whole, preferred_element_type=jnp.float32)
    row = lax.broadcasted_iota(jnp.int32, (SLOT // 8, KW), 0)
    col = lax.broadcasted_iota(jnp.int32, (SLOT // 8, KW), 1)
    pick = (col == row * GRP_ROWS + 8).astype(jnp.bfloat16)
    ninth = jnp.dot(pick, whole, preferred_element_type=jnp.float32).astype(jnp.bfloat16)
    row = lax.broadcasted_iota(jnp.int32, (SLOT, 128), 0)
    col = lax.broadcasted_iota(jnp.int32, (SLOT, 128), 1)
    pieces = []
    for s in range(8):
        pick = ((row == col - 64 + s * TAIL) & (col >= 64) & (col < 64 + TAIL)).astype(jnp.bfloat16)
        pieces.append(
            jnp.dot(ninth, pick, preferred_element_type=jnp.float32).astype(jnp.bfloat16)
        )
    pieces = jnp.concatenate(pieces, axis=0)
    row = lax.broadcasted_iota(jnp.int32, (SLOT, SLOT), 0)
    col = lax.broadcasted_iota(jnp.int32, (SLOT, SLOT), 1)
    pick = (col == (row & 7) * 64 + lax.shift_right_logical(row, 3)).astype(jnp.bfloat16)
    tail = jnp.dot(pick, pieces, preferred_element_type=jnp.float32)
    out_ref[:, :384] = first[:, :384].astype(jnp.bfloat16)
    out_ref[:, 384:] = (first[:, 384:] + tail).astype(jnp.bfloat16)


def down_grad(info, limits, blocks, hidden):
    return pl.pallas_call(
        down_kernel,
        out_shape=(
            jax.ShapeDtypeStruct((SLOT, SLOT), jnp.bfloat16),
            jax.ShapeDtypeStruct((KW, TOK), jnp.bfloat16),
        ),
        in_specs=[smem()] + [vmem()] * 7,
        out_specs=(vmem(), vmem()),
        scratch_shapes=[
            pltpu.VMEM((ROWS, PAIR), jnp.bfloat16),
            pltpu.VMEM((KW, CHIPS * PAIR), jnp.bfloat16),
            pltpu.VMEM((KW, SLOT), jnp.bfloat16),
        ],
        compiler_params=pltpu.CompilerParams(vmem_limit_bytes=20 * MIB),
        name="down_grad",
    )(info, limits, *blocks, hidden)


def added(*terms):
    total = terms[0].astype(jnp.float32)
    for term in terms[1:]:
        total = total + term.astype(jnp.float32)
    return total.astype(jnp.bfloat16)


def group_part(latent, queries, out_grad, hidden, doc_ids, clip_limits):
    position = lax.axis_index("ctx")
    core = position % 2
    info = jnp.stack([position // 2, core]).astype(jnp.int32)
    keys = pack(latent[0].T, doc_ids)
    near = chip_shift(keys, 1, 1)
    next_near = chip_shift(keys, 2, 2)
    query_rows = queries[0].reshape(QH, KW)
    third = chip_shift(keys, 3, 3)
    far_keys, info = lax.optimization_barrier((keys, info))
    fourth = chip_shift(far_keys, 4, 4)
    near, grads = lax.optimization_barrier((near, out_grad))
    grad_rows = grads[0].reshape(QH, LATENT)
    rows, cols = query_views(query_rows, grad_rows)
    own = jnp.stack([keys, near, next_near, third, fourth])
    own, rows, cols, info = lax.optimization_barrier((own, rows, cols, info))
    par = core_swap(own)
    send, mixed = attention(info, own, par, scores_of(own, rows), rows, cols)
    keep, mid = kept(info, own, par, mixed, cols)

    arrived = core_swap(send)
    far = chip_shift(added(keep[0], arrived[0]), 2, -2)
    close = chip_shift(added(keep[1], arrived[1]), 1, -1)
    mine = added(mid, far, close)
    total = added(mine, core_swap(mine))

    one = chip_shift(total, 1, -1)
    two = chip_shift(total, 2, -2)
    three = chip_shift(one, 2, -2)
    half = jnp.where(core == 0, two[:, :TOK], two[:, TOK:])
    four = chip_shift(half, 2, -2)
    one, two, three = lax.optimization_barrier((one, two, three))
    nearer = jnp.stack([one, two])
    nearer_par = core_swap(nearer)
    farther = jnp.concatenate([three, four], axis=1)
    blocks = [total, nearer, farther, nearer_par, core_swap(farther)]
    chunks, own_grad = down_grad(info, clip_limits, blocks, hidden[0].T)
    return own_grad, chunks


def on_device(latent, queries, out_grad, hidden, doc_ids, clip_limits):
    own_grad, chunks = group_part(latent, queries, out_grad, hidden, doc_ids, clip_limits)
    groups = lax.axis_size("grp")
    chunks = chunks.reshape(groups, SLOT // groups, SLOT)
    chunks = lax.all_to_all(chunks, "grp", 0, 0, tiled=True)
    mine = jnp.sum(chunks.astype(jnp.float32), axis=0)
    width = hidden.shape[2]
    ninth = mine[:, width : width + TAIL].reshape(1, width)
    weight_grad = jnp.concatenate([mine[:, :width], ninth], axis=0)
    return own_grad.T[None], weight_grad


def solution(mesh):
    return jax.shard_map(
        on_device,
        mesh=mesh,
        in_specs=(
            P("grp", "ctx", None),
            P("grp", "ctx", None),
            P("grp", "ctx", None),
            P("grp", None, "ctx"),
            P("grp", "ctx"),
            P("grp", None),
        ),
        out_specs=(P("grp", "ctx", None), P("grp", "ctx")),
        check_vma=False,
    )
```
